256 devices in a mesh: group: 8 (over x, core), seq: 32 (over y, z).
Axes of the slice: x: 4, y: 4, z: 8, core: 2. Of those that a mesh axis runs over, the one named last changes fastest.
Arguments:
- tokens: bfloat16 [16, 32768, 1024], P('group', 'seq'), may hold values from -24 to 24
- slot_params: bfloat16 [1024, 256], replicated, may hold values from -1 to 1
- w_up: bfloat16 [1024, 262144], P(None, ('group', 'seq')), may hold values from -0.1875 to 0.1875
- w_down: bfloat16 [262144, 1024], P(('group', 'seq')), may hold values from -0.375 to 0.375
Outputs:
- mixed: bfloat16 [16, 32768, 1024], P('group', 'seq')
The draws below stay inside these ranges and needn't reach their ends.
All inputs are finite; a program needn't handle non-finite values.
Results may differ from the reference program's by a relative error of at most 0.012.
Values may be sent and summed in bfloat16 or wider, within the bound.
No kernel may reach another device: no remote copies, remote signals or barrier semaphores. Data moves between devices by JAX's collectives and lax.ppermute only.
A program may use at most 192 MiB of HBM per device.

```python
import jax
import jax.numpy as jnp
from jax import lax

D = 1024
FF = 4096
SLOT_P = 4
SEQLEN = 32768
CLIPS = 16
EXPERTS = 64
SLOTS = 256


def slot_frame(key):
    frame_key = jax.random.fold_in(key, 11)
    sign_key, noise_key = jax.random.split(frame_key)
    common_width = D // 2
    feature = jnp.arange(D)
    in_common = (feature < common_width).astype(jnp.float32)
    sign_row = jnp.where(jax.random.bernoulli(sign_key, 0.5, (D,)), 1.0, -1.0).astype(jnp.float32)
    common = in_common * sign_row * 0.75
    specific = jax.random.normal(noise_key, (D, SLOTS), jnp.float32) * (4.0 / D ** 0.5)
    specific = jnp.clip(specific, -1.0, 1.0) * (1.0 - in_common)[:, None]
    return (common, specific, in_common)


def draw_slot_params(key, part):
    common, specific, in_common = slot_frame(key)
    return jnp.clip(common[:, None] + specific, -1.0, 1.0).astype(jnp.bfloat16)


def draw_tokens(key, part):
    common, specific, in_common = slot_frame(key)
    key = jax.random.fold_in(key, 2)
    normal_key = jax.random.fold_in(key, 0)
    order_key = jax.random.fold_in(key, 5)
    jitter_key = jax.random.fold_in(key, 6)
    common_width = D // 2
    order = jax.random.permutation(order_key, CLIPS).astype(jnp.float32)
    jitter = jax.random.uniform(jitter_key, (CLIPS,), jnp.float32, 0.0, 1.0)
    level = -160.0 + 420.0 * (order + jitter) / CLIPS
    offset = level[:, None] * common[None, :] / (common_width * 0.5625)
    feature_std = 0.15 * in_common + (1.0 - in_common)
    values = jnp.clip(jax.random.normal(normal_key, (CLIPS, SEQLEN, D), jnp.float32), -6.0, 6.0)
    values = values * feature_std[None, None, :] + offset[:, None, :]
    values = jnp.clip(values, -24.0, 24.0)
    return values.astype(jnp.bfloat16)


def with_spikes(entries, key, source, target, shards_of, factor):
    owner, partner = [(jnp.arange(entries.shape[axis_at]) // (entries.shape[axis_at] // shards_of)).reshape([-1 if axis == axis_at else 1 for axis in range(entries.ndim)]) for axis_at in (source, target)]
    chosen = jax.random.permutation(key, shards_of)[partner]
    strong = (owner == chosen) | (owner == (partner + shards_of // 2) % shards_of)
    return jnp.where(strong, factor * entries, entries)


def steps_of(rng, shape, cuts, smallest, top_value):
    def one(axis_at, parts):
        steps = jax.random.uniform(jax.random.fold_in(jax.random.fold_in(rng, 6), axis_at), (parts,), jnp.float32, smallest / len(cuts), top_value / len(cuts))
        return jnp.repeat(jnp.exp(steps), shape[axis_at] // parts).reshape((-1,) + (1,) * (len(shape) - axis_at - 1))

    gain = one(*cuts[0])
    for cut in cuts[1:]:
        gain = gain * one(*cut)
    return gain


def centred(own_key, shape, width, most, cuts=(), kind=jnp.bfloat16):
    entries = width * jax.random.normal(own_key, shape, jnp.float32)
    if cuts:
        entries = entries * steps_of(own_key, shape, cuts, -0.22, 0.18)
    return jnp.clip(entries, -most, most).astype(kind)


def bell_draw_with(stream_key, shape, scale, most, cuts, heavy, kind=jnp.bfloat16):
    values = scale * jax.random.normal(stream_key, shape, jnp.float32)
    if cuts:
        values = values * steps_of(stream_key, shape, cuts, -0.22, 0.18)
    return jnp.clip(with_spikes(values, jax.random.fold_in(stream_key, 3), *heavy), -most, most).astype(kind)


def setup_inputs(seed: int = 0) -> dict:
    streams_of = jax.random.split(jax.random.key(seed), 5)
    return {
        "tokens": draw_tokens(jax.random.fold_in(streams_of[4], 71), 0),
        "slot_params": draw_slot_params(jax.random.fold_in(streams_of[4], 71), 0),
        "w_up": centred(streams_of[2], (D, EXPERTS * FF), D ** -0.5, 0.1875, ((1, 256),)),
        "w_down": bell_draw_with(streams_of[3], (EXPERTS * FF, D), FF ** -0.5, 0.375, ((0, 256),), (0, 1, 256, 6.0)),
    }


def reference(tokens, slot_params, w_up, w_down):
    def per_clip(clip_rows):
        logits = jnp.dot(clip_rows, slot_params, preferred_element_type=jnp.float32)
        col_peak = jnp.max(logits, axis=0)
        spread = jnp.exp(logits - col_peak[None, :])
        col_total = jnp.sum(spread, axis=0)
        summed = jnp.dot(spread.astype(jnp.bfloat16).T, clip_rows, preferred_element_type=jnp.float32)
        slot_in = (summed / col_total[:, None]).astype(jnp.bfloat16)
        combine = jax.nn.softmax(logits, axis=1).astype(jnp.bfloat16)
        return slot_in, combine

    slot_in, combine = lax.map(per_clip, tokens)
    grouped = slot_in.reshape(CLIPS, EXPERTS, SLOT_P, D)

    def per_expert(index):
        inputs = lax.dynamic_index_in_dim(grouped, index, 1, keepdims=False).reshape(CLIPS * SLOT_P, D)
        start = (index * FF).astype(jnp.int32)
        first = lax.dynamic_slice_in_dim(w_up, start, FF, 1)
        second = lax.dynamic_slice_in_dim(w_down, start, FF, 0)
        hidden = jax.nn.gelu(jnp.dot(inputs, first, preferred_element_type=jnp.float32)).astype(jnp.bfloat16)
        result = jnp.dot(hidden, second, preferred_element_type=jnp.float32).astype(jnp.bfloat16)
        return result.reshape(CLIPS, SLOT_P, D)

    expert_out = lax.map(per_expert, jnp.arange(EXPERTS, dtype=jnp.int32))
    slot_out = jnp.transpose(expert_out, (1, 0, 2, 3)).reshape(CLIPS, SLOTS, D)

    def per_mix(pair):
        weights, outputs = pair
        return jnp.dot(weights, outputs, preferred_element_type=jnp.float32).astype(jnp.bfloat16)

    return lax.map(per_mix, (combine, slot_out))
```

```python
import functools

import jax
import jax.numpy as jnp
from jax import lax
from jax.experimental import pallas as pl
from jax.experimental.pallas import tpu as pltpu
from jax.sharding import Mesh
from jax.sharding import PartitionSpec as P

F32 = jnp.float32
BF16 = jnp.bfloat16
SLOT_P = 4
STAT = 128
MIB = 1 << 20


def vmem():
    return pl.BlockSpec(memory_space=pltpu.VMEM)


def params(mib=48):
    return pltpu.CompilerParams(vmem_limit_bytes=mib * MIB)


def device_order(slot_params, groups, ny, nz):
    slots = slot_params.shape[1]
    y = lax.axis_index("y")
    z = lax.axis_index("zh") * lax.axis_size("quarter") + lax.axis_index("quarter")
    row = lax.broadcasted_iota(jnp.int32, (slots, slots), 0)
    col = lax.broadcasted_iota(jnp.int32, (slots, slots), 1)
    at_y = (col // (nz * groups) + y) % ny
    at_z = (col // groups % nz + z) % nz
    perm = (row == (col % groups * ny + at_y) * nz + at_z).astype(F32).astype(BF16)
    return jnp.dot(slot_params, perm, preferred_element_type=F32).astype(BF16)


def gather_kernel(groups, ny, nz, tok_ref, sp_ref, *refs):
    out_refs, tick_ref = refs[:-1], refs[-1]
    tok = tok_ref[0]
    logits = jnp.dot(tok, device_order(sp_ref[...], groups, ny, nz), preferred_element_type=F32)
    peak = jnp.max(logits, axis=0, keepdims=True)
    spread = jnp.exp(logits - peak)
    total = jnp.sum(spread, axis=0, keepdims=True)
    summed = lax.dot_general(
        spread.astype(BF16), tok, (((0,), (0,)), ((), ())), preferred_element_type=F32
    )
    slots = logits.shape[1]
    both = jnp.concatenate([total, peak + jnp.log(total), jnp.zeros((6, slots), F32)], axis=0)
    cols = both.T
    wide = jnp.concatenate([summed / cols[:, 0:1], pack(cols[:, 1:2])], axis=1)
    wide = wide.reshape(ny, nz, groups, wide.shape[1]).astype(BF16)
    for i in range(ny):
        out_refs[i][:, 0] = wide[i]
    tick_ref[0] = both


def combine_kernel(groups, ny, nz, tok_ref, sp_ref, tick_ref, out_ref):
    logits = jnp.dot(tok_ref[0], device_order(sp_ref[...], groups, ny, nz), preferred_element_type=F32)
    spread = jnp.exp(logits - jnp.max(logits, axis=1, keepdims=True))
    out_ref[0] = (spread / jnp.sum(spread, axis=1, keepdims=True)).astype(BF16)


def pack(lse):
    hi = lse.astype(BF16).astype(F32)
    mid = (lse - hi).astype(BF16).astype(F32)
    low = lse - hi - mid
    lane = lax.broadcasted_iota(jnp.int32, lse.shape[:-1] + (STAT,), lse.ndim - 1)
    return jnp.where(lane == 0, hi, jnp.where(lane == 1, mid, jnp.where(lane == 2, low, 0.0)))


def merged(width, wides):
    lses = []
    for wide in wides:
        stat = wide[..., width:].astype(F32)
        lses.append(stat[..., 0:1] + stat[..., 1:2] + stat[..., 2:3])
    peak = functools.reduce(jnp.maximum, lses)
    weights = [jnp.exp(lse - peak) for lse in lses]
    total = sum(weights)
    mean = sum(wide[..., :width].astype(F32) * (w / total) for wide, w in zip(wides, weights))
    return mean, peak + jnp.log(total)


def halfway_kernel(width, ny, *refs):
    in_refs, out_refs = refs[:ny], refs[ny:]
    for k, out_ref in enumerate(out_refs):
        mean, lse = merged(width, [r[k] for r in in_refs])
        out_ref[...] = jnp.concatenate([mean, pack(lse)], axis=-1).astype(BF16)


def merge_kernel(width, *refs):
    in_refs, out_ref = refs[:-1], refs[-1]
    clips, groups = in_refs[0].shape[:2]
    acc, _ = merged(width, [r[...] for r in in_refs])
    for g in range(groups):
        rows = jnp.concatenate([acc[c, g : g + 1] for c in range(clips)], axis=0).astype(BF16)
        for q in range(SLOT_P):
            out_ref[g * SLOT_P + q] = rows


def expert_kernel(x_ref, up_ref, down_ref, out_ref):
    parts, clips, width = x_ref.shape
    x = x_ref[...].astype(F32).reshape(parts * clips, width).astype(BF16)
    hidden = jax.nn.gelu(jnp.dot(x, up_ref[...], preferred_element_type=F32)).astype(BF16)
    out = jnp.dot(hidden, down_ref[...], preferred_element_type=F32)
    out_ref[...] = out.reshape(parts, clips, width).astype(BF16)


def total_kernel(x_ref, out_ref):
    parts, clips, width = x_ref.shape
    x = x_ref[...].astype(F32).reshape(parts // SLOT_P, SLOT_P, clips, width)
    total = jnp.sum(x, axis=1)
    for c in range(clips):
        out_ref[c] = jnp.concatenate(
            [total[g, c : c + 1] for g in range(parts // SLOT_P)], axis=0
        ).astype(BF16)


def stack_kernel(*refs):
    for k, ref in enumerate(refs[:-1]):
        refs[-1][k] = ref[...]


def mix_kernel(comb_ref, *refs):
    slot_refs, out_ref = refs[:-1], refs[-1]
    nz, _, groups, width = slot_refs[0].shape
    slots = [r[:, 0].astype(F32).reshape(nz * groups, width) for r in slot_refs]
    slots = jnp.concatenate(slots, axis=0).astype(BF16)
    out_ref[0] = jnp.dot(comb_ref[0], slots, preferred_element_type=F32).astype(BF16)


def shards(tokens, slot_params, w_up, w_down):
    clips, length, width = tokens.shape
    slots = slot_params.shape[1]
    groups = lax.axis_size("group")
    around = ("zh", "quarter")
    ny, nz = lax.axis_size("y"), lax.axis_size(around)
    sharers = ("group", "quarter")

    def name(f, *a):
        def body(*refs):
            f(*a, *refs)

        return body

    def shift(x, axis, n, k):
        return lax.ppermute(x, axis, [(i, (i + k) % n) for i in range(n)])

    tok_spec = pl.BlockSpec((1, length, width), lambda c: (c, 0, 0))
    sp_spec = pl.BlockSpec((width, slots), lambda c: (0, 0))
    tick_spec = pl.BlockSpec((1, 8, slots), lambda c: (c, 0, 0))
    wide = width + STAT
    *means, tick = pl.pallas_call(
        name(gather_kernel, groups, ny, nz),
        grid=(clips,),
        in_specs=[tok_spec, sp_spec],
        out_specs=[pl.BlockSpec((nz, 1, groups, wide), lambda c: (0, c, 0, 0))] * ny + [tick_spec],
        out_shape=[jax.ShapeDtypeStruct((nz, clips, groups, wide), BF16)] * ny
        + [jax.ShapeDtypeStruct((clips, 8, slots), F32)],
        compiler_params=params(56),
        name="gather",
    )(tokens, slot_params)
    arrived = [means[0]] + [shift(means[k], "y", ny, k) for k in range(1, ny)]
    combine = pl.pallas_call(
        name(combine_kernel, groups, ny, nz),
        grid=(clips,),
        in_specs=[tok_spec, sp_spec, tick_spec],
        out_specs=pl.BlockSpec((1, length, slots), lambda c: (c, 0, 0)),
        out_shape=jax.ShapeDtypeStruct((clips, length, slots), BF16),
        compiler_params=params(56),
        cost_estimate=pl.CostEstimate(
            flops=2 * clips * length * width * slots,
            bytes_accessed=2 * clips * length * (width + slots),
            transcendentals=clips * length * slots,
        ),
        name="combine",
    )(tokens, slot_params, tick)
    halfway = pl.pallas_call(
        name(halfway_kernel, width, ny),
        in_specs=[vmem()] * ny,
        out_specs=[vmem()] * nz,
        out_shape=[jax.ShapeDtypeStruct((clips, groups, wide), BF16)] * nz,
        compiler_params=params(),
        name="halfway",
    )(*arrived)
    arrived = [halfway[0]] + [shift(halfway[k], around, nz, k) for k in range(1, nz)]
    slot_in = pl.pallas_call(
        name(merge_kernel, width),
        in_specs=[vmem()] * nz,
        out_specs=vmem(),
        out_shape=jax.ShapeDtypeStruct((groups * SLOT_P, clips, width), BF16),
        compiler_params=params(),
        name="merge",
    )(*arrived)
    own = lax.all_to_all(slot_in, sharers, 0, 0, tiled=True)
    partial = pl.pallas_call(
        expert_kernel,
        in_specs=[vmem()] * 3,
        out_specs=vmem(),
        out_shape=jax.ShapeDtypeStruct((groups * SLOT_P, clips, width), BF16),
        compiler_params=params(),
        name="expert",
    )(own, w_up, w_down)
    back = lax.all_to_all(partial, sharers, 0, 0, tiled=True)
    slot_out = pl.pallas_call(
        total_kernel,
        in_specs=[vmem()],
        out_specs=vmem(),
        out_shape=jax.ShapeDtypeStruct((clips, groups, width), BF16),
        compiler_params=params(),
        name="total",
    )(back)
    ring = pl.pallas_call(
        stack_kernel,
        in_specs=[vmem()] * nz,
        out_specs=vmem(),
        out_shape=jax.ShapeDtypeStruct((nz, clips, groups, width), BF16),
        compiler_params=params(),
        name="stack",
    )(slot_out, *[shift(slot_out, around, nz, -k) for k in range(1, nz)])
    rings = [ring] + [shift(ring, "y", ny, -k) for k in range(1, ny)]
    half = length // 2
    return pl.pallas_call(
        mix_kernel,
        grid=(clips, 2),
        in_specs=[
            pl.BlockSpec((1, half, slots), lambda c, t: (c, t, 0)),
        ]
        + [pl.BlockSpec((nz, 1, groups, width), lambda c, t: (0, c, 0, 0))] * ny,
        out_specs=pl.BlockSpec((1, half, width), lambda c, t: (c, t, 0)),
        out_shape=jax.ShapeDtypeStruct((clips, length, width), BF16),
        compiler_params=params(),
        name="mix",
    )(combine, *rings)


def solution(mesh):
    groups, n = mesh.devices.shape
    split = Mesh(mesh.devices.reshape(groups, 4, n // (4 * SLOT_P), SLOT_P), ("group", "y", "zh", "quarter"))
    seq = ("y", "zh", "quarter")
    everyone = ("group",) + seq
    placed = (P("group", seq, None), P(), P(None, everyone), P(everyone, None))
    return jax.shard_map(
        shards, mesh=split, in_specs=placed, out_specs=P("group", seq, None), check_vma=False
    )
```

```python
import functools

import jax
import jax.numpy as jnp
from jax import lax
from jax.experimental import pallas as pl
from jax.experimental.pallas import tpu as pltpu
from jax.sharding import Mesh
from jax.sharding import PartitionSpec as P

F32 = jnp.float32
BF16 = jnp.bfloat16
SLOT_P = 4
STAT = 128
STEPS = 4
MIB = 1 << 20
BIG = 52
ROWS = (((1,), (1,)), ((), ()))


def vmem():
    return pl.BlockSpec(memory_space=pltpu.VMEM)


def params(mib=48):
    return pltpu.CompilerParams(vmem_limit_bytes=mib * MIB)


def name(f, *a):
    def body(*refs):
        f(*a, *refs)

    return body


def first_member(group, nz):
    return group % 2 * (nz // 2)


def device_order(slot_params, groups, ny, nz):
    slots = slot_params.shape[1]
    row = lax.broadcasted_iota(jnp.int32, (slots, 1), 0)
    at_y = (row // (nz * groups) + lax.axis_index("y")) % ny
    at_z = (row // groups + first_member(lax.axis_index("group"), nz)) % nz
    slot = (row % groups * ny + at_y) * nz + at_z
    perm = (lax.broadcasted_iota(jnp.int32, (slots, slots), 1) == slot).astype(F32).astype(BF16)
    return lax.dot_general(perm, slot_params, ROWS, preferred_element_type=F32).astype(BF16)


def pack(lse):
    hi = lse.astype(BF16).astype(F32)
    mid = (lse - hi).astype(BF16).astype(F32)
    low = lse - hi - mid
    lane = lax.broadcasted_iota(jnp.int32, lse.shape[:-1] + (STAT,), lse.ndim - 1)
    return jnp.where(lane == 0, hi, jnp.where(lane == 1, mid, jnp.where(lane == 2, low, 0.0)))


def gather_kernel(clip, groups, ny, nz, tok_hbm, sp_ref, *refs):
    out_refs, refs = refs[:ny], refs[ny:]
    tok_ref, logit_ref, sems = refs[-3:]
    rows = tok_ref.shape[0] // STEPS
    copies = []
    for i in range(STEPS):
        part = pl.ds(i * rows, rows)
        copies.append(pltpu.make_async_copy(tok_hbm.at[clip, part], tok_ref.at[part], sems.at[i]))
        copies[-1].start()
    if len(refs) == 4:
        refs[0][...] = device_order(sp_ref[...], groups, ny, nz)
        sp_ref = refs[0]
    for i in range(STEPS):
        copies[i].wait()
        part = slice(i * rows, (i + 1) * rows)
        logit_ref[:, part] = lax.dot_general(sp_ref[...], tok_ref[part], ROWS, preferred_element_type=F32)
    logits = logit_ref[...]
    peak = jnp.max(logits, axis=1, keepdims=True)
    spread = jnp.exp(logits - peak)
    total = jnp.sum(spread, axis=1, keepdims=True)
    summed = jnp.dot(spread.astype(BF16), tok_ref[...], preferred_element_type=F32)
    wide = jnp.concatenate([summed * (1.0 / total), pack(peak + jnp.log(total))], axis=1)
    wide = wide.reshape(ny, nz, groups, wide.shape[1]).astype(BF16)
    for i in range(ny):
        out_refs[i][...] = wide[i]


def combine_kernel(tok_ref, sp_ref, after_ref, out_ref, tick_ref):
    logits = lax.dot_general(tok_ref[0], sp_ref[...], ROWS, preferred_element_type=F32)
    spread = jnp.exp(logits - jnp.max(logits, axis=1, keepdims=True))
    out_ref[0] = (spread * (1.0 / jnp.sum(spread, axis=1, keepdims=True))).astype(BF16)
    tick_ref[...] = jnp.zeros_like(tick_ref)


def merged(width, wides):
    lses = []
    for wide in wides:
        stat = wide[..., width:].astype(F32)
        lses.append(stat[..., 0:1] + stat[..., 1:2] + stat[..., 2:3])
    peak = functools.reduce(jnp.maximum, lses)
    weights = [jnp.exp(lse - peak) for lse in lses]
    total = sum(weights)
    mean = sum(wide[..., :width].astype(F32) * (w / total) for wide, w in zip(wides, weights))
    return mean, peak + jnp.log(total)


def halfway_kernel(width, ny, *refs):
    in_refs, out_ref = refs[:-1], refs[-1]
    for k in range(out_ref.shape[0]):
        for c in range(out_ref.shape[1]):
            mean, lse = merged(width, [r[k] for r in in_refs[c * ny : (c + 1) * ny]])
            out_ref[k, c] = jnp.concatenate([mean, pack(lse)], axis=-1).astype(BF16)


def merge_kernel(width, in_ref, after_ref, out_ref):
    nz, clips, groups = in_ref.shape[:3]
    acc, _ = merged(width, [in_ref[k] for k in range(nz)])
    for g in range(groups):
        rows = jnp.concatenate([acc[c, g : g + 1] for c in range(clips)], axis=0).astype(BF16)
        for q in range(SLOT_P):
            out_ref[g * SLOT_P + q] = rows


def expert_kernel(x_ref, up_ref, down_ref, out_ref):
    parts, clips, width = x_ref.shape
    x = x_ref[...].astype(F32).reshape(parts * clips, width).astype(BF16)
    hidden = jax.nn.gelu(jnp.dot(x, up_ref[...], preferred_element_type=F32)).astype(BF16)
    out = jnp.dot(hidden, down_ref[...], preferred_element_type=F32)
    out_ref[...] = out.reshape(parts, clips, width).astype(BF16)


def total_kernel(x_ref, out_ref):
    parts, clips, width = x_ref.shape
    x = x_ref[...].astype(F32).reshape(parts // SLOT_P, SLOT_P, clips, width)
    total = jnp.sum(x, axis=1)
    for c in range(clips):
        rows = jnp.concatenate([total[g, c : c + 1] for g in range(parts // SLOT_P)], axis=0).astype(BF16)
        for k in range(out_ref.shape[0]):
            out_ref[k, c] = rows


def split_kernel(in_ref, *out_refs):
    nz, _, groups, width = in_ref.shape
    for c, ref in enumerate(out_refs):
        ref[...] = in_ref[:, c].astype(F32).reshape(nz * groups, width).astype(BF16)


def mix_kernel(ny, *refs):
    comb_ref, slot_refs, (out_ref, held) = refs[0], refs[1 : 1 + ny], refs[-2:]
    rows = slot_refs[0].shape[0]

    @pl.when(pl.program_id(0) == 0)
    def _():
        for i, r in enumerate(slot_refs):
            held[i * rows : (i + 1) * rows] = r[...]

    out_ref[0] = jnp.dot(comb_ref[0], held[...], preferred_element_type=F32).astype(BF16)


def shards(tokens, slot_params, w_up, w_down):
    clips, length, width = tokens.shape
    slots = slot_params.shape[1]
    groups = lax.axis_size("group")
    around = ("zh", "quarter")
    ny, nz = lax.axis_size("y"), lax.axis_size(around)
    sharers = ("group", "quarter")
    wide = width + STAT

    def shift(x, k):
        return lax.ppermute(x, "y", [(i, (i + k) % ny) for i in range(ny)])

    everyone = ("group", "y") + around
    starts = [g * ny * nz + y * nz for g in range(groups) for y in range(ny)]
    order = [[first_member(s // (ny * nz), nz) + j for j in range(nz)] for s in starts]
    circles = [[s + j % nz for j in o] for s, o in zip(starts, order)]

    def exchange_z(x):
        return lax.all_to_all(x, everyone, 0, 0, axis_index_groups=circles, tiled=True)

    def small(kernel, out, label, *operands):
        return pl.pallas_call(
            kernel,
            in_specs=[vmem()] * len(operands),
            out_specs=jax.tree.map(lambda _: vmem(), out),
            out_shape=out,
            compiler_params=params(),
            name=label,
        )(*operands)

    def gather(clip, sp):
        extra = [jax.ShapeDtypeStruct((slots, width), BF16)] if clip == 0 else []
        return pl.pallas_call(
            name(gather_kernel, clip, groups, ny, nz),
            in_specs=[pl.BlockSpec(memory_space=pl.ANY), vmem()],
            out_specs=[vmem()] * (ny + len(extra)),
            out_shape=[jax.ShapeDtypeStruct((nz, groups, wide), BF16)] * ny + extra,
            scratch_shapes=[
                pltpu.VMEM((length, width), BF16),
                pltpu.VMEM((slots, length), F32),
                pltpu.SemaphoreType.DMA((STEPS,)),
            ],
            compiler_params=params(BIG + 1 if clip == 0 else BIG),
            cost_estimate=pl.CostEstimate(
                flops=4 * length * width * slots,
                bytes_accessed=2 * length * width,
                transcendentals=length * slots,
            ),
            name=f"gather{clip}",
        )(tokens, sp)

    arrived = []
    ordered = slot_params
    for clip in range(clips):
        means = gather(clip, ordered)
        if clip == 0:
            ordered = means[ny]
        arrived += [means[0]] + [shift(means[k], k) for k in range(1, ny)]
    halfway = small(
        name(halfway_kernel, width, ny),
        jax.ShapeDtypeStruct((nz, clips, groups, wide), BF16),
        "halfway",
        *arrived,
    )
    arrived = exchange_z(halfway)
    half = length // 2
    combine, tick = pl.pallas_call(
        combine_kernel,
        grid=(clips, 2),
        in_specs=[
            pl.BlockSpec((1, half, width), lambda c, t: (c, t, 0)),
            pl.BlockSpec((slots, width), lambda c, t: (0, 0)),
            pl.BlockSpec((1, 1, groups, STAT), lambda c, t: (0, 0, 0, 0)),
        ],
        out_specs=[
            pl.BlockSpec((1, half, slots), lambda c, t: (c, t, 0)),
            pl.BlockSpec((8, STAT), lambda c, t: (0, 0)),
        ],
        out_shape=[
            jax.ShapeDtypeStruct((clips, length, slots), BF16),
            jax.ShapeDtypeStruct((8, STAT), F32),
        ],
        compiler_params=params(BIG),
        cost_estimate=pl.CostEstimate(
            flops=2 * clips * length * width * slots,
            bytes_accessed=2 * clips * length * (width + slots),
            transcendentals=clips * length * slots,
        ),
        name="combine",
    )(tokens, ordered, halfway)
    rows = jax.ShapeDtypeStruct((groups * SLOT_P, clips, width), BF16)
    slot_in = small(name(merge_kernel, width), rows, "merge", arrived, tick)
    own = lax.all_to_all(slot_in, sharers, 0, 0, tiled=True)
    partial = small(expert_kernel, rows, "expert", own, w_up, w_down)
    back = lax.all_to_all(partial, sharers, 0, 0, tiled=True)
    slot_out = small(
        total_kernel, jax.ShapeDtypeStruct((nz, clips, groups, width), BF16), "total", back
    )
    ring = exchange_z(slot_out)
    own = small(
        split_kernel, [jax.ShapeDtypeStruct((nz * groups, width), BF16)] * clips, "split", ring
    )
    above0, below1 = shift(own[0], -1), shift(own[1], 1)
    below0, above1 = shift(own[0], 1), shift(own[1], -1)
    far0, far1 = shift(above0, -1), shift(below1, 1)
    rings = [[own[0], above0, far0, below0], [own[1], above1, far1, below1]]
    steps = 2
    mixed = None
    for clip in range(clips):
        before = [] if mixed is None else [mixed]
        mixed = pl.pallas_call(
            name(mix_kernel, ny),
            grid=(steps,),
            in_specs=[pl.BlockSpec((1, length // steps, slots), lambda t, c=clip: (c, t, 0))]
            + [pl.BlockSpec((nz * groups, width), lambda t: (0, 0))] * ny
            + [pl.BlockSpec(memory_space=pl.ANY) for _ in before],
            out_specs=pl.BlockSpec((1, length // steps, width), lambda t, c=clip: (c, t, 0)),
            out_shape=jax.ShapeDtypeStruct((clips, length, width), BF16),
            scratch_shapes=[pltpu.VMEM((slots, width), BF16)],
            input_output_aliases={1 + ny: 0} if before else {},
            compiler_params=params(),
            cost_estimate=pl.CostEstimate(
                flops=2 * length * width * slots,
                bytes_accessed=2 * length * (width + slots),
                transcendentals=0,
            ),
            name=f"mix{clip}",
        )(combine, *rings[clip], *before)
    return mixed


def solution(mesh):
    groups, n = mesh.devices.shape
    split = Mesh(mesh.devices.reshape(groups, 4, n // (4 * SLOT_P), SLOT_P), ("group", "y", "zh", "quarter"))
    seq = ("y", "zh", "quarter")
    everyone = ("group",) + seq
    placed = (P("group", seq, None), P(), P(None, everyone), P(everyone, None))
    return jax.shard_map(
        shards, mesh=split, in_specs=placed, out_specs=P("group", seq, None), check_vma=False
    )
```

```python
import functools

import jax
import jax.numpy as jnp
from jax import lax
from jax.experimental import pallas as pl
from jax.experimental.pallas import tpu as pltpu
from jax.sharding import Mesh
from jax.sharding import PartitionSpec as P

F32 = jnp.float32
BF16 = jnp.bfloat16
SLOT_P = 4
STAT = 128
STEPS = 4
MIB = 1 << 20
BIG = 52


def vmem():
    return pl.BlockSpec(memory_space=pltpu.VMEM)


def anywhere():
    return pl.BlockSpec(memory_space=pl.ANY)


def params(mib=48):
    return pltpu.CompilerParams(vmem_limit_bytes=mib * MIB)


def name(f, *a):
    def body(*refs):
        f(*a, *refs)

    return body


def device_order(slot_params, groups, ny, nz):
    slots = slot_params.shape[1]
    col = lax.broadcasted_iota(jnp.int32, (1, slots), 1)
    at_y = (col // (nz * groups) + lax.axis_index("y")) % ny
    slot = (col % groups * ny + at_y) * nz + col // groups % nz
    perm = (lax.broadcasted_iota(jnp.int32, (slots, slots), 0) == slot).astype(F32).astype(BF16)
    return jnp.dot(slot_params, perm, preferred_element_type=F32).astype(BF16)


def pack(lse):
    hi = lse.astype(BF16).astype(F32)
    mid = (lse - hi).astype(BF16).astype(F32)
    low = lse - hi - mid
    lane = lax.broadcasted_iota(jnp.int32, lse.shape[:-1] + (STAT,), lse.ndim - 1)
    return jnp.where(lane == 0, hi, jnp.where(lane == 1, mid, jnp.where(lane == 2, low, 0.0)))


def gather_kernel(clip, groups, ny, nz, tok_hbm, sp_ref, *refs):
    out_refs, refs = refs[:ny], refs[ny:]
    ordered_ref, tok_ref, logit_ref, sems = refs[-4:]
    rows = tok_ref.shape[0] // STEPS
    copies = []
    first = pltpu.make_async_copy(sp_ref, ordered_ref, sems.at[STEPS])
    first.start()
    for i in range(STEPS):
        part = pl.ds(i * rows, rows)
        copies.append(pltpu.make_async_copy(tok_hbm.at[clip, part], tok_ref.at[part], sems.at[i]))
        copies[-1].start()
    first.wait()
    if clip == 0:
        refs[0][...] = device_order(ordered_ref[...], groups, ny, nz)
        ordered_ref = refs[0]
    peak = None
    for i in range(STEPS):
        copies[i].wait()
        part = slice(i * rows, (i + 1) * rows)
        logits = jnp.dot(tok_ref[part], ordered_ref[...], preferred_element_type=F32)
        logit_ref[part] = logits
        top = jnp.max(logits, axis=0, keepdims=True)
        peak = top if peak is None else jnp.maximum(peak, top)
    spread = jnp.exp(logit_ref[...] - peak)
    total = jnp.sum(spread, axis=0, keepdims=True)
    summed = lax.dot_general(
        spread.astype(BF16), tok_ref[...], (((0,), (0,)), ((), ())), preferred_element_type=F32
    )
    slots = total.shape[1]
    cols = jnp.concatenate([1.0 / total, peak + jnp.log(total), jnp.zeros((6, slots), F32)], axis=0).T
    wide = jnp.concatenate([summed * cols[:, 0:1], pack(cols[:, 1:2])], axis=1)
    wide = wide.reshape(ny, nz, groups, wide.shape[1]).astype(BF16)
    for i in range(ny):
        out_refs[i][...] = wide[i]


def combine_kernel(tok_ref, sp_ref, after_ref, out_ref, tick_ref):
    logits = jnp.dot(tok_ref[0], sp_ref[...], preferred_element_type=F32)
    spread = jnp.exp(logits - jnp.max(logits, axis=1, keepdims=True))
    out_ref[0] = (spread * (1.0 / jnp.sum(spread, axis=1, keepdims=True))).astype(BF16)
    tick_ref[...] = jnp.zeros_like(tick_ref)


def merged(width, wides):
    lses = []
    for wide in wides:
        stat = wide[..., width:].astype(F32)
        lses.append(stat[..., 0:1] + stat[..., 1:2] + stat[..., 2:3])
    peak = functools.reduce(jnp.maximum, lses)
    weights = [jnp.exp(lse - peak) for lse in lses]
    total = sum(weights)
    mean = sum(wide[..., :width].astype(F32) * (w / total) for wide, w in zip(wides, weights))
    return mean, peak + jnp.log(total)


def halfway_kernel(width, *refs):
    in_refs, out_ref = refs[:-2], refs[-1]
    for k in range(out_ref.shape[0]):
        mean, lse = merged(width, [r[k] for r in in_refs])
        out_ref[k] = jnp.concatenate([mean, pack(lse)], axis=-1).astype(BF16)


def both_kernel(width, *refs):
    in_refs, first_ref, out_ref = refs[:-2], refs[-2], refs[-1]
    for k in range(out_ref.shape[0]):
        out_ref[k, 0] = first_ref[k]
        mean, lse = merged(width, [r[k] for r in in_refs])
        out_ref[k, 1] = jnp.concatenate([mean, pack(lse)], axis=-1).astype(BF16)


def merge_kernel(width, in_ref, out_ref):
    nz, clips, groups = in_ref.shape[:3]
    acc, _ = merged(width, [in_ref[k] for k in range(nz)])
    for g in range(groups):
        rows = jnp.concatenate([acc[c, g : g + 1] for c in range(clips)], axis=0).astype(BF16)
        for q in range(SLOT_P):
            out_ref[g * SLOT_P + q] = rows


def expert_kernel(x_ref, up_ref, down_ref, out_ref):
    parts, clips, width = x_ref.shape
    x = x_ref[...].astype(F32).reshape(parts * clips, width).astype(BF16)
    hidden = jax.nn.gelu(jnp.dot(x, up_ref[...], preferred_element_type=F32)).astype(BF16)
    out = jnp.dot(hidden, down_ref[...], preferred_element_type=F32)
    out_ref[...] = out.reshape(parts, clips, width).astype(BF16)


def total_kernel(x_ref, out_ref):
    parts, clips, width = x_ref.shape
    x = x_ref[...].astype(F32).reshape(parts // SLOT_P, SLOT_P, clips, width)
    total = jnp.sum(x, axis=1)
    for c in range(clips):
        rows = jnp.concatenate([total[g, c : c + 1] for g in range(parts // SLOT_P)], axis=0).astype(BF16)
        for k in range(out_ref.shape[0]):
            out_ref[k, c] = rows


def split_kernel(in_ref, *out_refs):
    nz, _, groups, width = in_ref.shape
    for c, ref in enumerate(out_refs):
        ref[...] = in_ref[:, c].astype(F32).reshape(nz * groups, width).astype(BF16)


def mix_kernel(clip, ny, comb_ref, *refs):
    slot_refs, (out_hbm, held, buf, sems) = refs[:ny], refs[-4:]
    rows = slot_refs[0].shape[0]
    for i, r in enumerate(slot_refs):
        held[i * rows : (i + 1) * rows] = r[...]
    step = buf.shape[0] // STEPS
    copies = []
    for i in range(STEPS):
        part = pl.ds(i * step, step)
        buf[part] = jnp.dot(comb_ref[clip, part], held[...], preferred_element_type=F32).astype(BF16)
        copies.append(pltpu.make_async_copy(buf.at[part], out_hbm.at[clip, part], sems.at[i]))
        copies[-1].start()
    for copy in copies:
        copy.wait()


def shards(tokens, slot_params, w_up, w_down):
    clips, length, width = tokens.shape
    slots = slot_params.shape[1]
    groups = lax.axis_size("group")
    around = ("zh", "quarter")
    ny, nz = lax.axis_size("y"), lax.axis_size(around)
    sharers = ("group", "quarter")
    wide = width + STAT

    def shift(x, k):
        return lax.ppermute(x, "y", [(i, (i + k) % ny) for i in range(ny)])

    def small(kernel, out, label, *operands):
        return pl.pallas_call(
            kernel,
            in_specs=[vmem()] * len(operands),
            out_specs=jax.tree.map(lambda _: vmem(), out),
            out_shape=out,
            compiler_params=params(),
            name=label,
        )(*operands)

    def gather(clip, sp):
        extra = [jax.ShapeDtypeStruct((width, slots), BF16)] if clip == 0 else []
        return pl.pallas_call(
            name(gather_kernel, clip, groups, ny, nz),
            in_specs=[anywhere(), anywhere()],
            out_specs=[vmem()] * (ny + len(extra)),
            out_shape=[jax.ShapeDtypeStruct((nz, groups, wide), BF16)] * ny + extra,
            scratch_shapes=[
                pltpu.VMEM((width, slots), BF16),
                pltpu.VMEM((length, width), BF16),
                pltpu.VMEM((length, slots), F32),
                pltpu.SemaphoreType.DMA((STEPS + 1,)),
            ],
            compiler_params=params(BIG + 1),
            cost_estimate=pl.CostEstimate(
                flops=4 * length * width * slots,
                bytes_accessed=2 * length * width,
                transcendentals=length * slots,
            ),
            name=f"gather{clip}",
        )(tokens, sp)

    arrived = []
    ordered = slot_params
    for clip in range(clips):
        means = gather(clip, ordered)
        if clip == 0:
            ordered = means[ny]
        arrived += [means[0]] + [shift(means[k], k) for k in range(1, ny)]
    half = length // 2
    combine, tick = pl.pallas_call(
        combine_kernel,
        grid=(clips, 2),
        in_specs=[
            pl.BlockSpec((1, half, width), lambda c, t: (c, t, 0)),
            pl.BlockSpec((width, slots), lambda c, t: (0, 0)),
            pl.BlockSpec((1, groups, STAT), lambda c, t: (0, 0, 0)),
        ],
        out_specs=[
            pl.BlockSpec((1, half, slots), lambda c, t: (c, t, 0)),
            pl.BlockSpec((8, STAT), lambda c, t: (0, 0)),
        ],
        out_shape=[
            jax.ShapeDtypeStruct((clips, length, slots), BF16),
            jax.ShapeDtypeStruct((8, STAT), F32),
        ],
        compiler_params=params(BIG),
        cost_estimate=pl.CostEstimate(
            flops=2 * clips * length * width * slots,
            bytes_accessed=2 * clips * length * (width + slots),
            transcendentals=clips * length * slots,
        ),
        name="combine",
    )(tokens, ordered, arrived[-ny])
    assert clips == 2
    halfway = small(
        name(halfway_kernel, width),
        jax.ShapeDtypeStruct((nz, groups, wide), BF16),
        "halfway",
        *arrived[:ny],
        tick,
    )
    halfway = small(
        name(both_kernel, width),
        jax.ShapeDtypeStruct((nz, clips, groups, wide), BF16),
        "both",
        *arrived[ny:],
        halfway,
    )
    arrived = lax.all_to_all(halfway, around, 0, 0, tiled=True)
    rows = jax.ShapeDtypeStruct((groups * SLOT_P, clips, width), BF16)
    slot_in = small(name(merge_kernel, width), rows, "merge", arrived)
    own = lax.all_to_all(slot_in, sharers, 0, 0, tiled=True)
    partial = small(expert_kernel, rows, "expert", own, w_up, w_down)
    back = lax.all_to_all(partial, sharers, 0, 0, tiled=True)
    slot_out = small(
        total_kernel, jax.ShapeDtypeStruct((nz, clips, groups, width), BF16), "total", back
    )
    ring = lax.all_to_all(slot_out, around, 0, 0, tiled=True)
    rings = small(
        split_kernel, [jax.ShapeDtypeStruct((nz * groups, width), BF16)] * clips, "split", ring
    )
    rings = [[ring] + [shift(ring, -k) for k in range(1, ny)] for ring in rings]
    mixed = None
    for clip in range(clips):
        before = [] if mixed is None else [mixed]
        mixed = pl.pallas_call(
            name(mix_kernel, clip, ny),
            in_specs=[vmem()] * (1 + ny) + [anywhere() for _ in before],
            out_specs=anywhere(),
            out_shape=jax.ShapeDtypeStruct((clips, length, width), BF16),
            scratch_shapes=[
                pltpu.VMEM((slots, width), BF16),
                pltpu.VMEM((length, width), BF16),
                pltpu.SemaphoreType.DMA((STEPS,)),
            ],
            input_output_aliases={1 + ny: 0} if before else {},
            compiler_params=params(),
            cost_estimate=pl.CostEstimate(
                flops=2 * length * width * slots,
                bytes_accessed=2 * length * (width + slots),
                transcendentals=0,
            ),
            name=f"mix{clip}",
        )(combine, *rings[clip], *before)
    return mixed


def solution(mesh):
    groups, n = mesh.devices.shape
    split = Mesh(mesh.devices.reshape(groups, 4, n // (4 * SLOT_P), SLOT_P), ("group", "y", "zh", "quarter"))
    seq = ("y", "zh", "quarter")
    everyone = ("group",) + seq
    placed = (P("group", seq, None), P(), P(None, everyone), P(everyone, None))
    return jax.shard_map(
        shards, mesh=split, in_specs=placed, out_specs=P("group", seq, None), check_vma=False
    )
```

```python
import functools

import jax
import jax.numpy as jnp
from jax import lax
from jax.experimental import pallas as pl
from jax.experimental.pallas import tpu as pltpu
from jax.sharding import Mesh
from jax.sharding import PartitionSpec as P

F32 = jnp.float32
BF16 = jnp.bfloat16
SLOT_P = 4
STAT = 128
STEPS = 4
MIB = 1 << 20
BIG = 52
FAR_FIRST = (2, 1, 3)
FAR_LAST = (0, 1, 3, 2)


def vmem():
    return pl.BlockSpec(memory_space=pltpu.VMEM)


def anywhere():
    return pl.BlockSpec(memory_space=pl.ANY)


def params(mib=48):
    return pltpu.CompilerParams(vmem_limit_bytes=mib * MIB)


def name(f, *a):
    def body(*refs):
        f(*a, *refs)

    return body


def device_order(slot_params, groups, ny, nz):
    slots = slot_params.shape[1]
    col = lax.broadcasted_iota(jnp.int32, (1, slots), 1)
    at_y = (col // (nz * groups) + lax.axis_index("y")) % ny
    slot = (col % groups * ny + at_y) * nz + col // groups % nz
    perm = (lax.broadcasted_iota(jnp.int32, (slots, slots), 0) == slot).astype(F32).astype(BF16)
    return jnp.dot(slot_params, perm, preferred_element_type=F32).astype(BF16)


def pack(lse):
    hi = lse.astype(BF16).astype(F32)
    mid = (lse - hi).astype(BF16).astype(F32)
    low = lse - hi - mid
    lane = lax.broadcasted_iota(jnp.int32, lse.shape[:-1] + (STAT,), lse.ndim - 1)
    return jnp.where(lane == 0, hi, jnp.where(lane == 1, mid, jnp.where(lane == 2, low, 0.0)))


def gather_kernel(clip, groups, ny, nz, tok_hbm, sp_ref, *refs):
    out_refs, refs = refs[:ny], refs[ny:]
    ordered_ref, tok_ref, logit_ref, sems = refs[-4:]
    rows = tok_ref.shape[0] // STEPS
    copies = []
    first = pltpu.make_async_copy(sp_ref, ordered_ref, sems.at[STEPS])
    first.start()
    for i in range(STEPS):
        part = pl.ds(i * rows, rows)
        copies.append(pltpu.make_async_copy(tok_hbm.at[clip, part], tok_ref.at[part], sems.at[i]))
        copies[-1].start()
    first.wait()
    if clip == 0:
        refs[0][...] = device_order(ordered_ref[...], groups, ny, nz)
        ordered_ref = refs[0]
    peak = None
    for i in range(STEPS):
        copies[i].wait()
        part = slice(i * rows, (i + 1) * rows)
        logits = jnp.dot(tok_ref[part], ordered_ref[...], preferred_element_type=F32)
        logit_ref[part] = logits
        top = jnp.max(logits, axis=0, keepdims=True)
        peak = top if peak is None else jnp.maximum(peak, top)
    spread = jnp.exp(logit_ref[...] - peak)
    total = jnp.sum(spread, axis=0, keepdims=True)
    summed = lax.dot_general(
        spread.astype(BF16), tok_ref[...], (((0,), (0,)), ((), ())), preferred_element_type=F32
    )
    slots = total.shape[1]
    cols = jnp.concatenate([1.0 / total, peak + jnp.log(total), jnp.zeros((6, slots), F32)], axis=0).T
    wide = jnp.concatenate([summed * cols[:, 0:1], pack(cols[:, 1:2])], axis=1)
    wide = wide.reshape(ny, nz, groups, wide.shape[1]).astype(BF16)
    for i in range(ny):
        out_refs[i][...] = wide[i]


def combine_kernel(tok_ref, sp_ref, after_ref, out_ref, tick_ref):
    logits = jnp.dot(tok_ref[0], sp_ref[...], preferred_element_type=F32)
    spread = jnp.exp(logits - jnp.max(logits, axis=1, keepdims=True))
    out_ref[...] = (spread * (1.0 / jnp.sum(spread, axis=1, keepdims=True))).astype(BF16)
    tick_ref[...] = jnp.zeros_like(tick_ref)


def merged(width, wides):
    lses = []
    for wide in wides:
        stat = wide[..., width:].astype(F32)
        lses.append(stat[..., 0:1] + stat[..., 1:2] + stat[..., 2:3])
    peak = functools.reduce(jnp.maximum, lses)
    weights = [jnp.exp(lse - peak) for lse in lses]
    total = sum(weights)
    mean = sum(wide[..., :width].astype(F32) * (w / total) for wide, w in zip(wides, weights))
    return mean, peak + jnp.log(total)


def halfway_kernel(width, *refs):
    in_refs, out_ref = refs[:-2], refs[-1]
    for k in range(out_ref.shape[0]):
        mean, lse = merged(width, [r[k] for r in in_refs])
        out_ref[k] = jnp.concatenate([mean, pack(lse)], axis=-1).astype(BF16)


def both_kernel(width, *refs):
    in_refs, first_ref, out_ref = refs[:-2], refs[-2], refs[-1]
    for k in range(out_ref.shape[0]):
        out_ref[k, 0] = first_ref[k]
        mean, lse = merged(width, [r[k] for r in in_refs])
        out_ref[k, 1] = jnp.concatenate([mean, pack(lse)], axis=-1).astype(BF16)


def merge_kernel(width, in_ref, out_ref):
    nz, clips, groups = in_ref.shape[:3]
    acc, _ = merged(width, [in_ref[k] for k in range(nz)])
    for g in range(groups):
        rows = jnp.concatenate([acc[c, g : g + 1] for c in range(clips)], axis=0).astype(BF16)
        for q in range(SLOT_P):
            out_ref[g * SLOT_P + q] = rows


def expert_kernel(x_ref, up_ref, down_ref, out_ref):
    parts, clips, width = x_ref.shape
    x = x_ref[...].astype(F32).reshape(parts * clips, width).astype(BF16)
    hidden = jax.nn.gelu(jnp.dot(x, up_ref[...], preferred_element_type=F32)).astype(BF16)
    out = jnp.dot(hidden, down_ref[...], preferred_element_type=F32)
    out_ref[...] = out.reshape(parts, clips, width).astype(BF16)


def total_kernel(x_ref, out_ref):
    parts, clips, width = x_ref.shape
    x = x_ref[...].astype(F32).reshape(parts // SLOT_P, SLOT_P, clips, width)
    total = jnp.sum(x, axis=1)
    for c in range(clips):
        rows = jnp.concatenate([total[g, c : c + 1] for g in range(parts // SLOT_P)], axis=0).astype(BF16)
        for k in range(out_ref.shape[0]):
            out_ref[k, c] = rows


def split_kernel(in_ref, *out_refs):
    nz, _, groups, width = in_ref.shape
    for c, ref in enumerate(out_refs):
        ref[...] = in_ref[:, c].astype(F32).reshape(nz * groups, width).astype(BF16)


def mix_kernel(clip, ny, comb_ref, *refs):
    slot_refs, (out_hbm, held, buf, sems) = refs[:ny], refs[-4:]
    rows = slot_refs[0].shape[0]
    for i, r in zip(FAR_LAST, slot_refs):
        held[i * rows : (i + 1) * rows] = r[...]
    step = buf.shape[0] // STEPS
    copies = []
    for i in range(STEPS):
        part = pl.ds(i * step, step)
        buf[part] = jnp.dot(comb_ref[part], held[...], preferred_element_type=F32).astype(BF16)
        copies.append(pltpu.make_async_copy(buf.at[part], out_hbm.at[clip, part], sems.at[i]))
        copies[-1].start()
    for copy in copies:
        copy.wait()


def shards(tokens, slot_params, w_up, w_down):
    clips, length, width = tokens.shape
    slots = slot_params.shape[1]
    groups = lax.axis_size("group")
    around = ("zh", "quarter")
    ny, nz = lax.axis_size("y"), lax.axis_size(around)
    sharers = ("group", "quarter")
    wide = width + STAT

    def shift(x, k):
        return lax.ppermute(x, "y", [(i, (i + k) % ny) for i in range(ny)])

    def small(kernel, out, label, *operands):
        return pl.pallas_call(
            kernel,
            in_specs=[vmem()] * len(operands),
            out_specs=jax.tree.map(lambda _: vmem(), out),
            out_shape=out,
            compiler_params=params(),
            name=label,
        )(*operands)

    def gather(clip, sp):
        extra = [jax.ShapeDtypeStruct((width, slots), BF16)] if clip == 0 else []
        return pl.pallas_call(
            name(gather_kernel, clip, groups, ny, nz),
            in_specs=[anywhere(), anywhere()],
            out_specs=[vmem()] * (ny + len(extra)),
            out_shape=[jax.ShapeDtypeStruct((nz, groups, wide), BF16)] * ny + extra,
            scratch_shapes=[
                pltpu.VMEM((width, slots), BF16),
                pltpu.VMEM((length, width), BF16),
                pltpu.VMEM((length, slots), F32),
                pltpu.SemaphoreType.DMA((STEPS + 1,)),
            ],
            compiler_params=params(BIG + 1),
            cost_estimate=pl.CostEstimate(
                flops=4 * length * width * slots,
                bytes_accessed=2 * length * width,
                transcendentals=length * slots,
            ),
            name=f"gather{clip}",
        )(tokens, sp)

    def combine(clip, after):
        half = length // 2
        return pl.pallas_call(
            combine_kernel,
            grid=(2,),
            in_specs=[
                pl.BlockSpec((1, half, width), lambda t: (clip, t, 0)),
                pl.BlockSpec((width, slots), lambda t: (0, 0)),
                pl.BlockSpec((1,) * (after.ndim - 2) + (8, STAT), lambda t: (0,) * after.ndim),
            ],
            out_specs=[
                pl.BlockSpec((half, slots), lambda t: (t, 0)),
                pl.BlockSpec((8, STAT), lambda t: (0, 0)),
            ],
            out_shape=[
                jax.ShapeDtypeStruct((length, slots), BF16),
                jax.ShapeDtypeStruct((8, STAT), F32),
            ],
            compiler_params=params(BIG),
            cost_estimate=pl.CostEstimate(
                flops=2 * length * width * slots,
                bytes_accessed=2 * length * (width + slots),
                transcendentals=length * slots,
            ),
            name=f"combine{clip}",
        )(tokens, ordered, after)

    assert clips == 2 and ny == 4
    *means0, ordered = gather(0, slot_params)
    sent0 = {k: shift(means0[k], k) for k in FAR_FIRST}
    means1 = gather(1, ordered)
    sent1 = {k: shift(means1[k], k) for k in FAR_FIRST}
    arrived = [means0[0], *sent0.values(), means1[0], *sent1.values()]
    combine0, tick = combine(0, means1[0])
    halfway = small(
        name(halfway_kernel, width),
        jax.ShapeDtypeStruct((nz, groups, wide), BF16),
        "halfway",
        *arrived[:ny],
        tick,
    )
    halfway = small(
        name(both_kernel, width),
        jax.ShapeDtypeStruct((nz, clips, groups, wide), BF16),
        "both",
        *arrived[ny:],
        halfway,
    )
    arrived = lax.all_to_all(halfway, around, 0, 0, tiled=True)
    rows = jax.ShapeDtypeStruct((groups * SLOT_P, clips, width), BF16)
    slot_in = small(name(merge_kernel, width), rows, "merge", arrived)
    own = lax.all_to_all(slot_in, sharers, 0, 0, tiled=True)
    partial = small(expert_kernel, rows, "expert", own, w_up, w_down)
    back = lax.all_to_all(partial, sharers, 0, 0, tiled=True)
    slot_out = small(
        total_kernel, jax.ShapeDtypeStruct((nz, clips, groups, width), BF16), "total", back
    )
    ring = lax.all_to_all(slot_out, around, 0, 0, tiled=True)
    rings = small(
        split_kernel, [jax.ShapeDtypeStruct((nz * groups, width), BF16)] * clips, "split", ring
    )
    combines = [combine0, combine(1, rings[0])[0]]
    rings = [[shift(ring, -k) if k else ring for k in FAR_LAST] for ring in rings]
    mixed = None
    for clip in range(clips):
        before = [] if mixed is None else [mixed]
        mixed = pl.pallas_call(
            name(mix_kernel, clip, ny),
            in_specs=[vmem()] * (1 + ny) + [anywhere() for _ in before],
            out_specs=anywhere(),
            out_shape=jax.ShapeDtypeStruct((clips, length, width), BF16),
            scratch_shapes=[
                pltpu.VMEM((slots, width), BF16),
                pltpu.VMEM((length, width), BF16),
                pltpu.SemaphoreType.DMA((STEPS,)),
            ],
            input_output_aliases={1 + ny: 0} if before else {},
            compiler_params=params(),
            cost_estimate=pl.CostEstimate(
                flops=2 * length * width * slots,
                bytes_accessed=2 * length * (width + slots),
                transcendentals=0,
            ),
            name=f"mix{clip}",
        )(combines[clip], *rings[clip], *before)
    return mixed


def solution(mesh):
    groups, n = mesh.devices.shape
    split = Mesh(mesh.devices.reshape(groups, 4, n // (4 * SLOT_P), SLOT_P), ("group", "y", "zh", "quarter"))
    seq = ("y", "zh", "quarter")
    everyone = ("group",) + seq
    placed = (P("group", seq, None), P(), P(None, everyone), P(everyone, None))
    return jax.shard_map(
        shards, mesh=split, in_specs=placed, out_specs=P("group", seq, None), check_vma=False
    )
```

```python
import functools

import jax
import jax.numpy as jnp
from jax import lax
from jax.experimental import pallas as pl
from jax.experimental.pallas import tpu as pltpu
from jax.sharding import Mesh
from jax.sharding import PartitionSpec as P

F32 = jnp.float32
BF16 = jnp.bfloat16
SLOT_P = 4
LANES = 128
STAT = LANES
STAT_ROWS = 16
STEPS = 4
MIB = 1 << 20
BIG = 52
FAR_FIRST = (2, 1, 3)
FAR_LAST = (0, 1, 3, 2)


def vmem():
    return pl.BlockSpec(memory_space=pltpu.VMEM)


def anywhere():
    return pl.BlockSpec(memory_space=pl.ANY)


def params(mib=48):
    return pltpu.CompilerParams(vmem_limit_bytes=mib * MIB)


def name(f, *a):
    def body(*refs):
        f(*a, *refs)

    return body


def device_order(slot_params, groups, ny, nz):
    slots = slot_params.shape[1]
    col = lax.broadcasted_iota(jnp.int32, (1, slots), 1)
    at_y = (col // (nz * groups) + lax.axis_index("y")) % ny
    slot = (col % groups * ny + at_y) * nz + col // groups % nz
    perm = (lax.broadcasted_iota(jnp.int32, (slots, slots), 0) == slot).astype(F32).astype(BF16)
    return jnp.dot(slot_params, perm, preferred_element_type=F32).astype(BF16)


def thirds(lse):
    hi = lse.astype(BF16).astype(F32)
    mid = (lse - hi).astype(BF16).astype(F32)
    return hi, mid, lse - hi - mid


def pack(lse):
    hi, mid, low = thirds(lse)
    lane = lax.broadcasted_iota(jnp.int32, lse.shape[:-1] + (STAT,), lse.ndim - 1)
    return jnp.where(lane == 0, hi, jnp.where(lane == 1, mid, jnp.where(lane == 2, low, 0.0)))


def gather_kernel(clip, groups, ny, nz, tok_hbm, sp_ref, *refs):
    out_refs, refs = refs[:ny], refs[ny:]
    ordered_ref, tok_ref, logit_ref, sems = refs[-4:]
    rows = tok_ref.shape[0] // STEPS
    copies = []
    first = pltpu.make_async_copy(sp_ref, ordered_ref, sems.at[STEPS])
    first.start()
    for i in range(STEPS):
        part = pl.ds(i * rows, rows)
        copies.append(pltpu.make_async_copy(tok_hbm.at[clip, part], tok_ref.at[part], sems.at[i]))
        copies[-1].start()
    first.wait()
    if clip == 0:
        refs[0][...] = device_order(ordered_ref[...], groups, ny, nz)
        ordered_ref = refs[0]
    peak = None
    for i in range(STEPS):
        copies[i].wait()
        part = slice(i * rows, (i + 1) * rows)
        logits = jnp.dot(tok_ref[part], ordered_ref[...], preferred_element_type=F32)
        logit_ref[part] = logits
        top = jnp.max(logits, axis=0, keepdims=True)
        peak = top if peak is None else jnp.maximum(peak, top)
    spread = jnp.exp(logit_ref[...] - peak)
    total = jnp.sum(spread, axis=0, keepdims=True)
    summed = lax.dot_general(
        spread.astype(BF16), tok_ref[...], (((0,), (0,)), ((), ())), preferred_element_type=F32
    )
    slots = total.shape[1]
    cols = jnp.concatenate([1.0 / total, jnp.zeros((7, slots), F32)], axis=0).T
    mean = (summed * cols[:, 0:1]).astype(BF16)
    stat = jnp.concatenate([*thirds(peak + jnp.log(total)), jnp.zeros((13, slots), F32)], axis=0).astype(BF16)
    rows = nz * groups
    for i in range(ny):
        block = mean[i * rows : (i + 1) * rows]
        tiles = block.shape[1] // LANES
        for t in range(tiles):
            out_refs[i][t * rows : (t + 1) * rows] = block[:, t * LANES : (t + 1) * LANES]
        at = i * rows // LANES * LANES
        out_refs[i][tiles * rows :] = stat[:, at : at + LANES]


def combine_kernel(tok_ref, sp_ref, after_ref, out_ref, tick_ref):
    logits = jnp.dot(tok_ref[0], sp_ref[...], preferred_element_type=F32)
    spread = jnp.exp(logits - jnp.max(logits, axis=1, keepdims=True))
    out_ref[...] = (spread * (1.0 / jnp.sum(spread, axis=1, keepdims=True))).astype(BF16)
    tick_ref[...] = jnp.zeros_like(tick_ref)


def merged(width, wides):
    lses = []
    for wide in wides:
        stat = wide[..., width:].astype(F32)
        lses.append(stat[..., 0:1] + stat[..., 1:2] + stat[..., 2:3])
    peak = functools.reduce(jnp.maximum, lses)
    weights = [jnp.exp(lse - peak) for lse in lses]
    total = sum(weights)
    mean = sum(wide[..., :width].astype(F32) * (w / total) for wide, w in zip(wides, weights))
    return mean, peak + jnp.log(total)


def along_y(rows, in_refs, store):
    tiles = (in_refs[0].shape[0] - STAT_ROWS) // rows
    lses = []
    for k, ref in zip((0,) + FAR_FIRST, in_refs):
        at = k * rows % LANES
        stat = ref[tiles * rows :].astype(F32).T[at : at + rows]
        lses.append(stat[:, 0:1] + stat[:, 1:2] + stat[:, 2:3])
    peak = functools.reduce(jnp.maximum, lses)
    weights = [jnp.exp(lse - peak) for lse in lses]
    total = sum(weights)
    weights = [w / total for w in weights]
    for t in range(tiles):
        part = slice(t * rows, (t + 1) * rows)
        store(t, sum(ref[part].astype(F32) * w for ref, w in zip(in_refs, weights)))
    store(tiles, pack(peak + jnp.log(total)))


def halfway_kernel(*refs):
    in_refs, out_ref = refs[:-2], refs[-1]
    nz, groups = out_ref.shape[:2]

    def store(t, x):
        out_ref[:, :, t * LANES : (t + 1) * LANES] = x.reshape(nz, groups, LANES).astype(BF16)

    along_y(nz * groups, in_refs, store)


def both_kernel(*refs):
    in_refs, first_ref, out_ref = refs[:-2], refs[-2], refs[-1]
    nz, _, groups = out_ref.shape[:3]

    def store(t, x):
        out_ref[:, 1, :, t * LANES : (t + 1) * LANES] = x.reshape(nz, groups, LANES).astype(BF16)

    out_ref[:, 0] = first_ref[...]
    along_y(nz * groups, in_refs, store)


def merge_kernel(width, in_ref, out_ref):
    nz, clips, groups = in_ref.shape[:3]
    acc, _ = merged(width, [in_ref[k] for k in range(nz)])
    for g in range(groups):
        rows = jnp.concatenate([acc[c, g : g + 1] for c in range(clips)], axis=0).astype(BF16)
        for q in range(SLOT_P):
            out_ref[g * SLOT_P + q] = rows


def expert_kernel(x_ref, up_ref, down_ref, out_ref):
    parts, clips, width = x_ref.shape
    x = x_ref[...].astype(F32).reshape(parts * clips, width).astype(BF16)
    hidden = jax.nn.gelu(jnp.dot(x, up_ref[...], preferred_element_type=F32)).astype(BF16)
    out = jnp.dot(hidden, down_ref[...], preferred_element_type=F32)
    out_ref[...] = out.reshape(parts, clips, width).astype(BF16)


def total_kernel(x_ref, out_ref):
    parts, clips, width = x_ref.shape
    x = x_ref[...].astype(F32).reshape(parts // SLOT_P, SLOT_P, clips, width)
    total = jnp.sum(x, axis=1)
    for c in range(clips):
        rows = jnp.concatenate([total[g, c : c + 1] for g in range(parts // SLOT_P)], axis=0).astype(BF16)
        for k in range(out_ref.shape[0]):
            out_ref[k, c] = rows


def split_kernel(in_ref, *out_refs):
    nz, _, groups, width = in_ref.shape
    for c, ref in enumerate(out_refs):
        ref[...] = in_ref[:, c].astype(F32).reshape(nz * groups, width).astype(BF16)


def mix_kernel(clip, ny, comb_ref, *refs):
    slot_refs, (out_hbm, held, buf, sems) = refs[:ny], refs[-4:]
    rows = slot_refs[0].shape[0]
    for i, r in zip(FAR_LAST, slot_refs):
        held[i * rows : (i + 1) * rows] = r[...]
    step = buf.shape[0] // STEPS
    copies = []
    for i in range(STEPS):
        part = pl.ds(i * step, step)
        buf[part] = jnp.dot(comb_ref[part], held[...], preferred_element_type=F32).astype(BF16)
        copies.append(pltpu.make_async_copy(buf.at[part], out_hbm.at[clip, part], sems.at[i]))
        copies[-1].start()
    for copy in copies:
        copy.wait()


def shards(tokens, slot_params, w_up, w_down):
    clips, length, width = tokens.shape
    slots = slot_params.shape[1]
    groups = lax.axis_size("group")
    around = ("zh", "quarter")
    ny, nz = lax.axis_size("y"), lax.axis_size(around)
    sharers = ("group", "quarter")
    wide = width + STAT

    def shift(x, k):
        return lax.ppermute(x, "y", [(i, (i + k) % ny) for i in range(ny)])

    def small(kernel, out, label, *operands):
        return pl.pallas_call(
            kernel,
            in_specs=[vmem()] * len(operands),
            out_specs=jax.tree.map(lambda _: vmem(), out),
            out_shape=out,
            compiler_params=params(),
            name=label,
        )(*operands)

    def gather(clip, sp):
        extra = [jax.ShapeDtypeStruct((width, slots), BF16)] if clip == 0 else []
        return pl.pallas_call(
            name(gather_kernel, clip, groups, ny, nz),
            in_specs=[anywhere(), anywhere()],
            out_specs=[vmem()] * (ny + len(extra)),
            out_shape=[jax.ShapeDtypeStruct((nz * groups * (width // LANES) + STAT_ROWS, LANES), BF16)] * ny + extra,
            scratch_shapes=[
                pltpu.VMEM((width, slots), BF16),
                pltpu.VMEM((length, width), BF16),
                pltpu.VMEM((length, slots), F32),
                pltpu.SemaphoreType.DMA((STEPS + 1,)),
            ],
            compiler_params=params(BIG + 1),
            cost_estimate=pl.CostEstimate(
                flops=4 * length * width * slots,
                bytes_accessed=2 * length * width,
                transcendentals=length * slots,
            ),
            name=f"gather{clip}",
        )(tokens, sp)

    def combine(clip, after):
        half = length // 2
        return pl.pallas_call(
            combine_kernel,
            grid=(2,),
            in_specs=[
                pl.BlockSpec((1, half, width), lambda t: (clip, t, 0)),
                pl.BlockSpec((width, slots), lambda t: (0, 0)),
                pl.BlockSpec((1,) * (after.ndim - 2) + (8, STAT), lambda t: (0,) * after.ndim),
            ],
            out_specs=[
                pl.BlockSpec((half, slots), lambda t: (t, 0)),
                pl.BlockSpec((8, STAT), lambda t: (0, 0)),
            ],
            out_shape=[
                jax.ShapeDtypeStruct((length, slots), BF16),
                jax.ShapeDtypeStruct((8, STAT), F32),
            ],
            compiler_params=params(BIG),
            cost_estimate=pl.CostEstimate(
                flops=2 * length * width * slots,
                bytes_accessed=2 * length * (width + slots),
                transcendentals=length * slots,
            ),
            name=f"combine{clip}",
        )(tokens, ordered, after)

    assert clips == 2 and ny == 4
    *means0, ordered = gather(0, slot_params)
    sent0 = {k: shift(means0[k], k) for k in FAR_FIRST}
    means1 = gather(1, ordered)
    sent1 = {k: shift(means1[k], k) for k in FAR_FIRST}
    arrived = [means0[0], *sent0.values(), means1[0], *sent1.values()]
    combine0, tick = combine(0, means1[0])
    combine1, tick = combine(1, tick)
    halfway = small(
        halfway_kernel,
        jax.ShapeDtypeStruct((nz, groups, wide), BF16),
        "halfway",
        *arrived[:ny],
        tick,
    )
    halfway = small(
        both_kernel,
        jax.ShapeDtypeStruct((nz, clips, groups, wide), BF16),
        "both",
        *arrived[ny:],
        halfway,
    )
    arrived = lax.all_to_all(halfway, around, 0, 0, tiled=True)
    rows = jax.ShapeDtypeStruct((groups * SLOT_P, clips, width), BF16)
    slot_in = small(name(merge_kernel, width), rows, "merge", arrived)
    own = lax.all_to_all(slot_in, sharers, 0, 0, tiled=True)
    partial = small(expert_kernel, rows, "expert", own, w_up, w_down)
    back = lax.all_to_all(partial, sharers, 0, 0, tiled=True)
    slot_out = small(
        total_kernel, jax.ShapeDtypeStruct((nz, clips, groups, width), BF16), "total", back
    )
    ring = lax.all_to_all(slot_out, around, 0, 0, tiled=True)
    rings = small(
        split_kernel, [jax.ShapeDtypeStruct((nz * groups, width), BF16)] * clips, "split", ring
    )
    combines = [combine0, combine1]
    rings = [[shift(ring, -k) if k else ring for k in FAR_LAST] for ring in rings]
    mixed = None
    for clip in range(clips):
        before = [] if mixed is None else [mixed]
        mixed = pl.pallas_call(
            name(mix_kernel, clip, ny),
            in_specs=[vmem()] * (1 + ny) + [anywhere() for _ in before],
            out_specs=anywhere(),
            out_shape=jax.ShapeDtypeStruct((clips, length, width), BF16),
            scratch_shapes=[
                pltpu.VMEM((slots, width), BF16),
                pltpu.VMEM((length, width), BF16),
                pltpu.SemaphoreType.DMA((STEPS,)),
            ],
            input_output_aliases={1 + ny: 0} if before else {},
            compiler_params=params(),
            cost_estimate=pl.CostEstimate(
                flops=2 * length * width * slots,
                bytes_accessed=2 * length * (width + slots),
                transcendentals=0,
            ),
            name=f"mix{clip}",
        )(combines[clip], *rings[clip], *before)
    return mixed


def solution(mesh):
    groups, n = mesh.devices.shape
    split = Mesh(mesh.devices.reshape(groups, 4, n // (4 * SLOT_P), SLOT_P), ("group", "y", "zh", "quarter"))
    seq = ("y", "zh", "quarter")
    everyone = ("group",) + seq
    placed = (P("group", seq, None), P(), P(None, everyone), P(everyone, None))
    return jax.shard_map(
        shards, mesh=split, in_specs=placed, out_specs=P("group", seq, None), check_vma=False
    )
```

```python
import functools

import jax
import jax.numpy as jnp
from jax import lax
from jax.experimental import pallas as pl
from jax.experimental.pallas import tpu as pltpu
from jax.sharding import Mesh
from jax.sharding import PartitionSpec as P

F32 = jnp.float32
BF16 = jnp.bfloat16
SLOT_P = 4
LANES = 128
STAT = LANES
STAT_ROWS = 16
STEPS = 4
MIB = 1 << 20
BIG = 52
LATE = 48
FAR_FIRST = (2, 1, 3)
FAR_LAST = (0, 1, 3, 2)


def vmem():
    return pl.BlockSpec(memory_space=pltpu.VMEM)


def anywhere():
    return pl.BlockSpec(memory_space=pl.ANY)


def params(mib=48):
    return pltpu.CompilerParams(vmem_limit_bytes=mib * MIB)


def name(f, *a):
    def body(*refs):
        f(*a, *refs)

    return body


def device_order(slot_params, groups, ny, nz):
    slots = slot_params.shape[1]
    col = lax.broadcasted_iota(jnp.int32, (1, slots), 1)
    at_y = (col // (nz * groups) + lax.axis_index("y")) % ny
    slot = (col % groups * ny + at_y) * nz + col // groups % nz
    perm = (lax.broadcasted_iota(jnp.int32, (slots, slots), 0) == slot).astype(F32).astype(BF16)
    return jnp.dot(slot_params, perm, preferred_element_type=F32).astype(BF16)


def thirds(lse):
    hi = lse.astype(BF16).astype(F32)
    mid = (lse - hi).astype(BF16).astype(F32)
    return hi, mid, lse - hi - mid


def pack(lse):
    hi, mid, low = thirds(lse)
    lane = lax.broadcasted_iota(jnp.int32, lse.shape[:-1] + (STAT,), lse.ndim - 1)
    return jnp.where(lane == 0, hi, jnp.where(lane == 1, mid, jnp.where(lane == 2, low, 0.0)))


def gather_kernel(clip, groups, ny, nz, tok_hbm, sp_ref, *refs):
    out_refs, refs = refs[:ny], refs[ny:]
    ordered_ref, tok_ref, logit_ref, sems = refs[-4:]
    rows = tok_ref.shape[0] // STEPS
    copies = []
    first = pltpu.make_async_copy(sp_ref, ordered_ref, sems.at[STEPS])
    first.start()
    for i in range(STEPS):
        part = pl.ds(i * rows, rows)
        copies.append(pltpu.make_async_copy(tok_hbm.at[clip, part], tok_ref.at[part], sems.at[i]))
        copies[-1].start()
    first.wait()
    if clip == 0:
        refs[0][...] = device_order(ordered_ref[...], groups, ny, nz)
        ordered_ref = refs[0]
    peak = None
    for i in range(STEPS):
        copies[i].wait()
        part = slice(i * rows, (i + 1) * rows)
        logits = jnp.dot(tok_ref[part], ordered_ref[...], preferred_element_type=F32)
        logit_ref[part] = logits
        top = jnp.max(logits, axis=0, keepdims=True)
        peak = top if peak is None else jnp.maximum(peak, top)
    spread = jnp.exp(logit_ref[...] - peak)
    total = jnp.sum(spread, axis=0, keepdims=True)
    summed = lax.dot_general(
        spread.astype(BF16), tok_ref[...], (((0,), (0,)), ((), ())), preferred_element_type=F32
    )
    slots = total.shape[1]
    cols = jnp.concatenate([1.0 / total, jnp.zeros((7, slots), F32)], axis=0).T
    mean = (summed * cols[:, 0:1]).astype(BF16)
    stat = jnp.concatenate([*thirds(peak + jnp.log(total)), jnp.zeros((13, slots), F32)], axis=0).astype(BF16)
    rows = nz * groups
    for i in range(ny):
        block = mean[i * rows : (i + 1) * rows]
        tiles = block.shape[1] // LANES
        for t in range(tiles):
            out_refs[i][t * rows : (t + 1) * rows] = block[:, t * LANES : (t + 1) * LANES]
        at = i * rows // LANES * LANES
        out_refs[i][tiles * rows :] = stat[:, at : at + LANES]


def combine_kernel(tok_ref, sp_ref, after_ref, out_ref, tick_ref):
    logits = jnp.dot(tok_ref[0], sp_ref[...], preferred_element_type=F32)
    spread = jnp.exp(logits - jnp.max(logits, axis=1, keepdims=True))
    out_ref[...] = (spread * (1.0 / jnp.sum(spread, axis=1, keepdims=True))).astype(BF16)
    tick_ref[...] = jnp.zeros_like(tick_ref)


def merged(width, wides):
    lses = []
    for wide in wides:
        stat = wide[..., width:].astype(F32)
        lses.append(stat[..., 0:1] + stat[..., 1:2] + stat[..., 2:3])
    peak = functools.reduce(jnp.maximum, lses)
    weights = [jnp.exp(lse - peak) for lse in lses]
    total = sum(weights)
    mean = sum(wide[..., :width].astype(F32) * (w / total) for wide, w in zip(wides, weights))
    return mean, peak + jnp.log(total)


def along_y(rows, in_refs, store):
    tiles = (in_refs[0].shape[0] - STAT_ROWS) // rows
    lses = []
    for k, ref in zip((0,) + FAR_FIRST, in_refs):
        at = k * rows % LANES
        stat = ref[tiles * rows :].astype(F32).T[at : at + rows]
        lses.append(stat[:, 0:1] + stat[:, 1:2] + stat[:, 2:3])
    peak = functools.reduce(jnp.maximum, lses)
    weights = [jnp.exp(lse - peak) for lse in lses]
    total = sum(weights)
    weights = [w / total for w in weights]
    for t in range(tiles):
        part = slice(t * rows, (t + 1) * rows)
        store(t, sum(ref[part].astype(F32) * w for ref, w in zip(in_refs, weights)))
    store(tiles, pack(peak + jnp.log(total)))


def halfway_kernel(*refs):
    in_refs, out_ref = refs[:-2], refs[-1]
    nz, groups = out_ref.shape[:2]

    def store(t, x):
        out_ref[:, :, t * LANES : (t + 1) * LANES] = x.reshape(nz, groups, LANES).astype(BF16)

    along_y(nz * groups, in_refs, store)


def both_kernel(*refs):
    in_refs, first_ref, out_ref = refs[:-2], refs[-2], refs[-1]
    nz, _, groups = out_ref.shape[:3]

    def store(t, x):
        out_ref[:, 1, :, t * LANES : (t + 1) * LANES] = x.reshape(nz, groups, LANES).astype(BF16)

    out_ref[:, 0] = first_ref[...]
    along_y(nz * groups, in_refs, store)


def merge_kernel(width, in_ref, after_ref, out_ref):
    nz, clips, groups = in_ref.shape[:3]
    acc, _ = merged(width, [in_ref[k] for k in range(nz)])
    for g in range(groups):
        rows = jnp.concatenate([acc[c, g : g + 1] for c in range(clips)], axis=0).astype(BF16)
        for q in range(SLOT_P):
            out_ref[g * SLOT_P + q] = rows


def expert_kernel(x_ref, up_ref, down_ref, out_ref):
    parts, clips, width = x_ref.shape
    x = x_ref[...].astype(F32).reshape(parts * clips, width).astype(BF16)
    hidden = jax.nn.gelu(jnp.dot(x, up_ref[...], preferred_element_type=F32)).astype(BF16)
    out = jnp.dot(hidden, down_ref[...], preferred_element_type=F32)
    out_ref[...] = out.reshape(parts, clips, width).astype(BF16)


def total_kernel(x_ref, out_ref):
    parts, clips, width = x_ref.shape
    x = x_ref[...].astype(F32).reshape(parts // SLOT_P, SLOT_P, clips, width)
    total = jnp.sum(x, axis=1)
    for c in range(clips):
        rows = jnp.concatenate([total[g, c : c + 1] for g in range(parts // SLOT_P)], axis=0).astype(BF16)
        for k in range(out_ref.shape[0]):
            out_ref[k, c] = rows


def split_kernel(in_ref, *out_refs):
    nz, _, groups, width = in_ref.shape
    for c, ref in enumerate(out_refs):
        ref[...] = in_ref[:, c].astype(F32).reshape(nz * groups, width).astype(BF16)


def mix_kernel(clip, ny, comb_ref, *refs):
    slot_refs, (out_hbm, held, buf, sems) = refs[:ny], refs[-4:]
    rows = slot_refs[0].shape[0]
    for i, r in zip(FAR_LAST, slot_refs):
        held[i * rows : (i + 1) * rows] = r[...]
    step = buf.shape[0] // STEPS
    copies = []
    for i in range(STEPS):
        part = pl.ds(i * step, step)
        buf[part] = jnp.dot(comb_ref[part], held[...], preferred_element_type=F32).astype(BF16)
        copies.append(pltpu.make_async_copy(buf.at[part], out_hbm.at[clip, part], sems.at[i]))
        copies[-1].start()
    for copy in copies:
        copy.wait()


def shards(tokens, slot_params, w_up, w_down):
    clips, length, width = tokens.shape
    slots = slot_params.shape[1]
    groups = lax.axis_size("group")
    around = ("zh", "quarter")
    ny, nz = lax.axis_size("y"), lax.axis_size(around)
    sharers = ("group", "quarter")
    wide = width + STAT

    def shift(x, k):
        return lax.ppermute(x, "y", [(i, (i + k) % ny) for i in range(ny)])

    def small(kernel, out, label, *operands):
        return pl.pallas_call(
            kernel,
            in_specs=[vmem()] * len(operands),
            out_specs=jax.tree.map(lambda _: vmem(), out),
            out_shape=out,
            compiler_params=params(),
            name=label,
        )(*operands)

    def gather(clip, sp):
        extra = [jax.ShapeDtypeStruct((width, slots), BF16)] if clip == 0 else []
        return pl.pallas_call(
            name(gather_kernel, clip, groups, ny, nz),
            in_specs=[anywhere(), anywhere()],
            out_specs=[vmem()] * (ny + len(extra)),
            out_shape=[jax.ShapeDtypeStruct((nz * groups * (width // LANES) + STAT_ROWS, LANES), BF16)] * ny + extra,
            scratch_shapes=[
                pltpu.VMEM((width, slots), BF16),
                pltpu.VMEM((length, width), BF16),
                pltpu.VMEM((length, slots), F32),
                pltpu.SemaphoreType.DMA((STEPS + 1,)),
            ],
            compiler_params=params(BIG + 1),
            cost_estimate=pl.CostEstimate(
                flops=4 * length * width * slots,
                bytes_accessed=2 * length * width,
                transcendentals=length * slots,
            ),
            name=f"gather{clip}",
        )(tokens, sp)

    def combine(clip, after):
        half = length // 2
        return pl.pallas_call(
            combine_kernel,
            grid=(2,),
            in_specs=[
                pl.BlockSpec((1, half, width), lambda t: (clip, t, 0)),
                pl.BlockSpec((width, slots), lambda t: (0, 0)),
                pl.BlockSpec((1,) * (after.ndim - 2) + (8, STAT), lambda t: (0,) * after.ndim),
            ],
            out_specs=[
                pl.BlockSpec((half, slots), lambda t: (t, 0)),
                pl.BlockSpec((8, STAT), lambda t: (0, 0)),
            ],
            out_shape=[
                jax.ShapeDtypeStruct((length, slots), BF16),
                jax.ShapeDtypeStruct((8, STAT), F32),
            ],
            compiler_params=params(BIG if clip == 0 else LATE),
            cost_estimate=pl.CostEstimate(
                flops=2 * length * width * slots,
                bytes_accessed=2 * length * (width + slots),
                transcendentals=length * slots,
            ),
            name=f"combine{clip}",
        )(tokens, ordered, after)

    assert clips == 2 and ny == 4
    *means0, ordered = gather(0, slot_params)
    sent0 = {k: shift(means0[k], k) for k in FAR_FIRST}
    means1 = gather(1, ordered)
    sent1 = {k: shift(means1[k], k) for k in FAR_FIRST}
    arrived = [means0[0], *sent0.values(), means1[0], *sent1.values()]
    combine0, tick = combine(0, means1[0])
    halfway = small(
        halfway_kernel,
        jax.ShapeDtypeStruct((nz, groups, wide), BF16),
        "halfway",
        *arrived[:ny],
        tick,
    )
    halfway = small(
        both_kernel,
        jax.ShapeDtypeStruct((nz, clips, groups, wide), BF16),
        "both",
        *arrived[ny:],
        halfway,
    )
    arrived = lax.all_to_all(halfway, around, 0, 0, tiled=True)
    combine1, tick = combine(1, halfway)
    rows = jax.ShapeDtypeStruct((groups * SLOT_P, clips, width), BF16)
    slot_in = small(name(merge_kernel, width), rows, "merge", arrived, tick)
    own = lax.all_to_all(slot_in, sharers, 0, 0, tiled=True)
    partial = small(expert_kernel, rows, "expert", own, w_up, w_down)
    back = lax.all_to_all(partial, sharers, 0, 0, tiled=True)
    slot_out = small(
        total_kernel, jax.ShapeDtypeStruct((nz, clips, groups, width), BF16), "total", back
    )
    ring = lax.all_to_all(slot_out, around, 0, 0, tiled=True)
    rings = small(
        split_kernel, [jax.ShapeDtypeStruct((nz * groups, width), BF16)] * clips, "split", ring
    )
    combines = [combine0, combine1]
    rings = [[shift(ring, -k) if k else ring for k in FAR_LAST] for ring in rings]
    mixed = None
    for clip in range(clips):
        before = [] if mixed is None else [mixed]
        mixed = pl.pallas_call(
            name(mix_kernel, clip, ny),
            in_specs=[vmem()] * (1 + ny) + [anywhere() for _ in before],
            out_specs=anywhere(),
            out_shape=jax.ShapeDtypeStruct((clips, length, width), BF16),
            scratch_shapes=[
                pltpu.VMEM((slots, width), BF16),
                pltpu.VMEM((length, width), BF16),
                pltpu.SemaphoreType.DMA((STEPS,)),
            ],
            input_output_aliases={1 + ny: 0} if before else {},
            compiler_params=params(),
            cost_estimate=pl.CostEstimate(
                flops=2 * length * width * slots,
                bytes_accessed=2 * length * (width + slots),
                transcendentals=0,
            ),
            name=f"mix{clip}",
        )(combines[clip], *rings[clip], *before)
    return mixed


def solution(mesh):
    groups, n = mesh.devices.shape
    split = Mesh(mesh.devices.reshape(groups, 4, n // (4 * SLOT_P), SLOT_P), ("group", "y", "zh", "quarter"))
    seq = ("y", "zh", "quarter")
    everyone = ("group",) + seq
    placed = (P("group", seq, None), P(), P(None, everyone), P(everyone, None))
    return jax.shard_map(
        shards, mesh=split, in_specs=placed, out_specs=P("group", seq, None), check_vma=False
    )
```

```python
import functools

import jax
import jax.numpy as jnp
from jax import lax
from jax.experimental import pallas as pl
from jax.experimental.pallas import tpu as pltpu
from jax.sharding import Mesh
from jax.sharding import PartitionSpec as P

F32 = jnp.float32
BF16 = jnp.bfloat16
SLOT_P = 4
LANES = 128
STAT = LANES
STAT_ROWS = 16
STEPS = 4
MIB = 1 << 20
BIG = 52
LATE = 44
FAR_FIRST = (2, 1, 3)
FAR_LAST = (0, 1, 3, 2)


def vmem():
    return pl.BlockSpec(memory_space=pltpu.VMEM)


def anywhere():
    return pl.BlockSpec(memory_space=pl.ANY)


def params(mib=48):
    return pltpu.CompilerParams(vmem_limit_bytes=int(mib * MIB))


def name(f, *a):
    def body(*refs):
        f(*a, *refs)

    return body


def device_order(slot_params, groups, ny, nz):
    slots = slot_params.shape[1]
    col = lax.broadcasted_iota(jnp.int32, (1, slots), 1)
    at_y = (col // (nz * groups) + lax.axis_index("y")) % ny
    slot = (col % groups * ny + at_y) * nz + col // groups % nz
    perm = (lax.broadcasted_iota(jnp.int32, (slots, slots), 0) == slot).astype(F32).astype(BF16)
    return jnp.dot(slot_params, perm, preferred_element_type=F32).astype(BF16)


def thirds(lse):
    hi = lse.astype(BF16).astype(F32)
    mid = (lse - hi).astype(BF16).astype(F32)
    return hi, mid, lse - hi - mid


def pack(lse):
    hi, mid, low = thirds(lse)
    lane = lax.broadcasted_iota(jnp.int32, lse.shape[:-1] + (STAT,), lse.ndim - 1)
    return jnp.where(lane == 0, hi, jnp.where(lane == 1, mid, jnp.where(lane == 2, low, 0.0)))


def gather_kernel(clip, groups, ny, nz, tok_in, sp_ref, *refs):
    out_refs, refs = refs[:ny], refs[ny:]
    copies = []
    if clip == 0:
        ordered_ref, raw_ref, tok_ref, logit_ref, sems = refs
        rows = tok_ref.shape[0] // STEPS
        first = pltpu.make_async_copy(sp_ref, raw_ref, sems.at[STEPS])
        first.start()
        for i in range(STEPS):
            part = pl.ds(i * rows, rows)
            copies.append(pltpu.make_async_copy(tok_in.at[clip, part], tok_ref.at[part], sems.at[i]))
            copies[-1].start()
        first.wait()
        ordered_ref[...] = device_order(raw_ref[...], groups, ny, nz)
    else:
        ordered_ref, tok_ref, logit_ref = sp_ref, tok_in.at[clip], refs[0]
        rows = tok_ref.shape[0] // STEPS
    peak = None
    for i in range(STEPS):
        if copies:
            copies[i].wait()
        part = slice(i * rows, (i + 1) * rows)
        logits = jnp.dot(tok_ref[part], ordered_ref[...], preferred_element_type=F32)
        logit_ref[part] = logits
        top = jnp.max(logits, axis=0, keepdims=True)
        peak = top if peak is None else jnp.maximum(peak, top)
    spread = jnp.exp(logit_ref[...] - peak)
    total = jnp.sum(spread, axis=0, keepdims=True)
    summed = lax.dot_general(
        spread.astype(BF16), tok_ref[...], (((0,), (0,)), ((), ())), preferred_element_type=F32
    )
    slots = total.shape[1]
    cols = jnp.concatenate([1.0 / total, jnp.zeros((7, slots), F32)], axis=0).T
    mean = (summed * cols[:, 0:1]).astype(BF16)
    stat = jnp.concatenate([*thirds(peak + jnp.log(total)), jnp.zeros((13, slots), F32)], axis=0).astype(BF16)
    rows = nz * groups
    for i in range(ny):
        block = mean[i * rows : (i + 1) * rows]
        tiles = block.shape[1] // LANES
        for t in range(tiles):
            out_refs[i][t * rows : (t + 1) * rows] = block[:, t * LANES : (t + 1) * LANES]
        at = i * rows // LANES * LANES
        out_refs[i][tiles * rows :] = stat[:, at : at + LANES]


def combine_kernel(tok_ref, sp_ref, after_ref, out_ref, tick_ref):
    logits = jnp.dot(tok_ref[0], sp_ref[...], preferred_element_type=F32)
    spread = jnp.exp(logits - jnp.max(logits, axis=1, keepdims=True))
    out_ref[...] = (spread * (1.0 / jnp.sum(spread, axis=1, keepdims=True))).astype(BF16)
    tick_ref[...] = jnp.zeros_like(tick_ref)


def merged(width, wides):
    lses = []
    for wide in wides:
        stat = wide[..., width:].astype(F32)
        lses.append(stat[..., 0:1] + stat[..., 1:2] + stat[..., 2:3])
    peak = functools.reduce(jnp.maximum, lses)
    weights = [jnp.exp(lse - peak) for lse in lses]
    total = sum(weights)
    mean = sum(wide[..., :width].astype(F32) * (w / total) for wide, w in zip(wides, weights))
    return mean, peak + jnp.log(total)


def along_y(rows, in_refs, store):
    tiles = (in_refs[0].shape[0] - STAT_ROWS) // rows
    lses = []
    for k, ref in zip((0,) + FAR_FIRST, in_refs):
        at = k * rows % LANES
        stat = ref[tiles * rows :].astype(F32).T[at : at + rows]
        lses.append(stat[:, 0:1] + stat[:, 1:2] + stat[:, 2:3])
    peak = functools.reduce(jnp.maximum, lses)
    weights = [jnp.exp(lse - peak) for lse in lses]
    total = sum(weights)
    weights = [w / total for w in weights]
    for t in range(tiles):
        part = slice(t * rows, (t + 1) * rows)
        store(t, sum(ref[part].astype(F32) * w for ref, w in zip(in_refs, weights)))
    store(tiles, pack(peak + jnp.log(total)))


def halfway_kernel(*refs):
    in_refs, out_ref = refs[:-2], refs[-1]
    nz, groups = out_ref.shape[:2]

    def store(t, x):
        out_ref[:, :, t * LANES : (t + 1) * LANES] = x.reshape(nz, groups, LANES).astype(BF16)

    along_y(nz * groups, in_refs, store)


def both_kernel(*refs):
    in_refs, first_ref, out_ref = refs[:-2], refs[-2], refs[-1]
    nz, _, groups = out_ref.shape[:3]

    def store(t, x):
        out_ref[:, 1, :, t * LANES : (t + 1) * LANES] = x.reshape(nz, groups, LANES).astype(BF16)

    out_ref[:, 0] = first_ref[...]
    along_y(nz * groups, in_refs, store)


def merge_kernel(width, in_ref, out_ref):
    nz, clips, groups = in_ref.shape[:3]
    acc, _ = merged(width, [in_ref[k] for k in range(nz)])
    for g in range(groups):
        rows = jnp.concatenate([acc[c, g : g + 1] for c in range(clips)], axis=0).astype(BF16)
        for q in range(SLOT_P):
            out_ref[g * SLOT_P + q] = rows


def expert_kernel(x_ref, up_ref, down_ref, out_ref):
    parts, clips, width = x_ref.shape
    x = x_ref[...].astype(F32).reshape(parts * clips, width).astype(BF16)
    hidden = jax.nn.gelu(jnp.dot(x, up_ref[...], preferred_element_type=F32)).astype(BF16)
    out = jnp.dot(hidden, down_ref[...], preferred_element_type=F32)
    out_ref[...] = out.reshape(parts, clips, width).astype(BF16)


def total_kernel(x_ref, out_ref):
    parts, clips, width = x_ref.shape
    x = x_ref[...].astype(F32).reshape(parts // SLOT_P, SLOT_P, clips, width)
    total = jnp.sum(x, axis=1)
    for c in range(clips):
        rows = jnp.concatenate([total[g, c : c + 1] for g in range(parts // SLOT_P)], axis=0).astype(BF16)
        for k in range(out_ref.shape[0]):
            out_ref[k, c] = rows


def split_kernel(in_ref, *out_refs):
    nz, _, groups, width = in_ref.shape
    for c, ref in enumerate(out_refs):
        ref[...] = in_ref[:, c].astype(F32).reshape(nz * groups, width).astype(BF16)


def mix_kernel(clip, ny, comb_ref, *refs):
    slot_refs, (out_hbm, held, buf, sems) = refs[:ny], refs[-4:]
    rows = slot_refs[0].shape[0]
    for i, r in zip(FAR_LAST, slot_refs):
        held[i * rows : (i + 1) * rows] = r[...]
    step = buf.shape[0] // STEPS
    copies = []
    for i in range(STEPS):
        part = pl.ds(i * step, step)
        buf[part] = jnp.dot(comb_ref[part], held[...], preferred_element_type=F32).astype(BF16)
        copies.append(pltpu.make_async_copy(buf.at[part], out_hbm.at[clip, part], sems.at[i]))
        copies[-1].start()
    for copy in copies:
        copy.wait()


def shards(tokens, slot_params, w_up, w_down):
    clips, length, width = tokens.shape
    slots = slot_params.shape[1]
    groups = lax.axis_size("group")
    around = ("zh", "quarter")
    ny, nz = lax.axis_size("y"), lax.axis_size(around)
    sharers = ("group", "quarter")
    wide = width + STAT

    def shift(x, k):
        return lax.ppermute(x, "y", [(i, (i + k) % ny) for i in range(ny)])

    def small(kernel, out, label, *operands):
        return pl.pallas_call(
            kernel,
            in_specs=[vmem()] * len(operands),
            out_specs=jax.tree.map(lambda _: vmem(), out),
            out_shape=out,
            compiler_params=params(),
            name=label,
        )(*operands)

    def gather(clip, sp):
        extra = [jax.ShapeDtypeStruct((width, slots), BF16)] if clip == 0 else []
        return pl.pallas_call(
            name(gather_kernel, clip, groups, ny, nz),
            in_specs=[anywhere(), anywhere()] if clip == 0 else [vmem(), vmem()],
            out_specs=[vmem()] * (ny + len(extra)),
            out_shape=[jax.ShapeDtypeStruct((nz * groups * (width // LANES) + STAT_ROWS, LANES), BF16)] * ny + extra,
            scratch_shapes=[
                pltpu.VMEM((width, slots), BF16),
                pltpu.VMEM((length, width), BF16),
                pltpu.VMEM((length, slots), F32),
                pltpu.SemaphoreType.DMA((STEPS + 1,)),
            ]
            if clip == 0
            else [pltpu.VMEM((length, slots), F32)],
            compiler_params=params(BIG + 0.625 if clip == 0 else LATE),
            cost_estimate=pl.CostEstimate(
                flops=4 * length * width * slots,
                bytes_accessed=2 * length * width,
                transcendentals=length * slots,
            ),
            name=f"gather{clip}",
        )(tokens, sp)

    def combine(clip, after):
        half = length // 2
        return pl.pallas_call(
            combine_kernel,
            grid=(2,),
            in_specs=[
                pl.BlockSpec((1, half, width), lambda t: (clip, t, 0)),
                pl.BlockSpec((width, slots), lambda t: (0, 0)),
                pl.BlockSpec((1,) * (after.ndim - 2) + (8, STAT), lambda t: (0,) * after.ndim),
            ],
            out_specs=[
                pl.BlockSpec((half, slots), lambda t: (t, 0)),
                pl.BlockSpec((8, STAT), lambda t: (0, 0)),
            ],
            out_shape=[
                jax.ShapeDtypeStruct((length, slots), BF16),
                jax.ShapeDtypeStruct((8, STAT), F32),
            ],
            compiler_params=params(LATE),
            cost_estimate=pl.CostEstimate(
                flops=2 * length * width * slots,
                bytes_accessed=2 * length * (width + slots),
                transcendentals=length * slots,
            ),
            name=f"combine{clip}",
        )(tokens, ordered, after)

    assert clips == 2 and ny == 4
    *means0, ordered = gather(0, slot_params)
    sent0 = {k: shift(means0[k], k) for k in FAR_FIRST}
    means1 = gather(1, ordered)
    sent1 = {k: shift(means1[k], k) for k in FAR_FIRST}
    arrived = [means0[0], *sent0.values(), means1[0], *sent1.values()]
    combine0, tick = combine(0, means1[0])
    combine1, tick = combine(1, tick)
    halfway = small(
        halfway_kernel,
        jax.ShapeDtypeStruct((nz, groups, wide), BF16),
        "halfway",
        *arrived[:ny],
        tick,
    )
    halfway = small(
        both_kernel,
        jax.ShapeDtypeStruct((nz, clips, groups, wide), BF16),
        "both",
        *arrived[ny:],
        halfway,
    )
    arrived = lax.all_to_all(halfway, around, 0, 0, tiled=True)
    rows = jax.ShapeDtypeStruct((groups * SLOT_P, clips, width), BF16)
    slot_in = small(name(merge_kernel, width), rows, "merge", arrived)
    own = lax.all_to_all(slot_in, sharers, 0, 0, tiled=True)
    partial = small(expert_kernel, rows, "expert", own, w_up, w_down)
    back = lax.all_to_all(partial, sharers, 0, 0, tiled=True)
    slot_out = small(
        total_kernel, jax.ShapeDtypeStruct((nz, clips, groups, width), BF16), "total", back
    )
    ring = lax.all_to_all(slot_out, around, 0, 0, tiled=True)
    rings = small(
        split_kernel, [jax.ShapeDtypeStruct((nz * groups, width), BF16)] * clips, "split", ring
    )
    combines = [combine0, combine1]
    rings = [[shift(ring, -k) if k else ring for k in FAR_LAST] for ring in rings]
    mixed = None
    for clip in range(clips):
        before = [] if mixed is None else [mixed]
        mixed = pl.pallas_call(
            name(mix_kernel, clip, ny),
            in_specs=[vmem()] * (1 + ny) + [anywhere() for _ in before],
            out_specs=anywhere(),
            out_shape=jax.ShapeDtypeStruct((clips, length, width), BF16),
            scratch_shapes=[
                pltpu.VMEM((slots, width), BF16),
                pltpu.VMEM((length, width), BF16),
                pltpu.SemaphoreType.DMA((STEPS,)),
            ],
            input_output_aliases={1 + ny: 0} if before else {},
            compiler_params=params(),
            cost_estimate=pl.CostEstimate(
                flops=2 * length * width * slots,
                bytes_accessed=2 * length * (width + slots),
                transcendentals=0,
            ),
            name=f"mix{clip}",
        )(combines[clip], *rings[clip], *before)
    return mixed


def solution(mesh):
    groups, n = mesh.devices.shape
    split = Mesh(mesh.devices.reshape(groups, 4, n // (4 * SLOT_P), SLOT_P), ("group", "y", "zh", "quarter"))
    seq = ("y", "zh", "quarter")
    everyone = ("group",) + seq
    placed = (P("group", seq, None), P(), P(None, everyone), P(everyone, None))
    return jax.shard_map(
        shards, mesh=split, in_specs=placed, out_specs=P("group", seq, None), check_vma=False
    )
```

```python
import functools

import jax
import jax.numpy as jnp
from jax import lax
from jax.experimental import pallas as pl
from jax.experimental.pallas import tpu as pltpu
from jax.sharding import Mesh
from jax.sharding import PartitionSpec as P

F32 = jnp.float32
BF16 = jnp.bfloat16
SLOT_P = 4
LANES = 128
STAT = LANES
STAT_ROWS = 16
STEPS = 8
PIECES = 4
MIB = 1 << 20
BIG = 52
LATE = 44
FAR_FIRST = (2, 1, 3)
FAR_LAST = (0, 1, 3, 2)


def vmem():
    return pl.BlockSpec(memory_space=pltpu.VMEM)


def anywhere():
    return pl.BlockSpec(memory_space=pl.ANY)


def params(mib=48):
    return pltpu.CompilerParams(vmem_limit_bytes=int(mib * MIB))


def name(f, *a):
    def body(*refs):
        f(*a, *refs)

    return body


def device_order(slots, groups, ny, nz):
    col = lax.broadcasted_iota(jnp.int32, (1, slots), 1)
    at_y = (col // (nz * groups) + lax.axis_index("y")) % ny
    slot = (col % groups * ny + at_y) * nz + col // groups % nz
    return (lax.broadcasted_iota(jnp.int32, (slots, slots), 0) == slot).astype(F32).astype(BF16)


def thirds(lse):
    hi = lse.astype(BF16).astype(F32)
    mid = (lse - hi).astype(BF16).astype(F32)
    return hi, mid, lse - hi - mid


def pack(lse):
    hi, mid, low = thirds(lse)
    lane = lax.broadcasted_iota(jnp.int32, lse.shape[:-1] + (STAT,), lse.ndim - 1)
    return jnp.where(lane == 0, hi, jnp.where(lane == 1, mid, jnp.where(lane == 2, low, 0.0)))


def gather_kernel(clip, groups, ny, nz, tok_in, sp_ref, *refs):
    out_refs, refs = refs[:ny], refs[ny:]
    copies = []
    if clip == 0:
        ordered_ref, raw_ref, tok_ref, logit_ref, sems = refs
        rows = tok_ref.shape[0] // STEPS
        some = raw_ref.shape[0] // PIECES
        first = []
        for i in range(PIECES):
            part = pl.ds(i * some, some)
            first.append(pltpu.make_async_copy(sp_ref.at[part], raw_ref.at[part], sems.at[STEPS + i]))
            first[-1].start()
        for i in range(STEPS):
            part = pl.ds(i * rows, rows)
            copies.append(pltpu.make_async_copy(tok_in.at[clip, part], tok_ref.at[part], sems.at[i]))
            copies[-1].start()
        perm = device_order(raw_ref.shape[1], groups, ny, nz)
        for i in range(PIECES):
            first[i].wait()
            part = slice(i * some, (i + 1) * some)
            ordered_ref[part] = jnp.dot(raw_ref[part], perm, preferred_element_type=F32).astype(BF16)
    else:
        ordered_ref, tok_ref, logit_ref = sp_ref, tok_in.at[clip], refs[0]
        rows = tok_ref.shape[0] // STEPS
    peak = None
    for i in range(STEPS):
        if copies:
            copies[i].wait()
        part = slice(i * rows, (i + 1) * rows)
        logits = jnp.dot(tok_ref[part], ordered_ref[...], preferred_element_type=F32)
        logit_ref[part] = logits
        top = jnp.max(logits, axis=0, keepdims=True)
        peak = top if peak is None else jnp.maximum(peak, top)
    spread = jnp.exp(logit_ref[...] - peak)
    total = jnp.sum(spread, axis=0, keepdims=True)
    summed = lax.dot_general(
        spread.astype(BF16), tok_ref[...], (((0,), (0,)), ((), ())), preferred_element_type=F32
    )
    slots = total.shape[1]
    cols = jnp.concatenate([1.0 / total, jnp.zeros((7, slots), F32)], axis=0).T
    mean = (summed * cols[:, 0:1]).astype(BF16)
    stat = jnp.concatenate([*thirds(peak + jnp.log(total)), jnp.zeros((13, slots), F32)], axis=0).astype(BF16)
    rows = nz * groups
    for i in range(ny):
        block = mean[i * rows : (i + 1) * rows]
        tiles = block.shape[1] // LANES
        for t in range(tiles):
            out_refs[i][t * rows : (t + 1) * rows] = block[:, t * LANES : (t + 1) * LANES]
        at = i * rows // LANES * LANES
        out_refs[i][tiles * rows :] = stat[:, at : at + LANES]


def combine_kernel(tok_ref, sp_ref, after_ref, out_ref, tick_ref):
    logits = jnp.dot(tok_ref[0], sp_ref[...], preferred_element_type=F32)
    spread = jnp.exp(logits - jnp.max(logits, axis=1, keepdims=True))
    out_ref[...] = (spread * (1.0 / jnp.sum(spread, axis=1, keepdims=True))).astype(BF16)
    tick_ref[...] = jnp.zeros_like(tick_ref)


def merged(width, wides):
    lses = []
    for wide in wides:
        stat = wide[..., width:].astype(F32)
        lses.append(stat[..., 0:1] + stat[..., 1:2] + stat[..., 2:3])
    peak = functools.reduce(jnp.maximum, lses)
    weights = [jnp.exp(lse - peak) for lse in lses]
    total = sum(weights)
    mean = sum(wide[..., :width].astype(F32) * (w / total) for wide, w in zip(wides, weights))
    return mean, peak + jnp.log(total)


def along_y(rows, in_refs, store):
    tiles = (in_refs[0].shape[0] - STAT_ROWS) // rows
    lses = []
    for k, ref in zip((0,) + FAR_FIRST, in_refs):
        at = k * rows % LANES
        stat = ref[tiles * rows :].astype(F32).T[at : at + rows]
        lses.append(stat[:, 0:1] + stat[:, 1:2] + stat[:, 2:3])
    peak = functools.reduce(jnp.maximum, lses)
    weights = [jnp.exp(lse - peak) for lse in lses]
    total = sum(weights)
    weights = [w / total for w in weights]
    for t in range(tiles):
        part = slice(t * rows, (t + 1) * rows)
        store(t, sum(ref[part].astype(F32) * w for ref, w in zip(in_refs, weights)))
    store(tiles, pack(peak + jnp.log(total)))


def halfway_kernel(*refs):
    in_refs, out_ref = refs[:-2], refs[-1]
    nz, groups = out_ref.shape[:2]

    def store(t, x):
        out_ref[:, :, t * LANES : (t + 1) * LANES] = x.reshape(nz, groups, LANES).astype(BF16)

    along_y(nz * groups, in_refs, store)


def both_kernel(*refs):
    in_refs, first_ref, out_ref = refs[:-2], refs[-2], refs[-1]
    nz, _, groups = out_ref.shape[:3]

    def store(t, x):
        out_ref[:, 1, :, t * LANES : (t + 1) * LANES] = x.reshape(nz, groups, LANES).astype(BF16)

    out_ref[:, 0] = first_ref[...]
    along_y(nz * groups, in_refs, store)


def merge_kernel(width, in_ref, out_ref):
    nz, clips, groups = in_ref.shape[:3]
    acc, _ = merged(width, [in_ref[k] for k in range(nz)])
    for g in range(groups):
        rows = jnp.concatenate([acc[c, g : g + 1] for c in range(clips)], axis=0).astype(BF16)
        for q in range(SLOT_P):
            out_ref[g * SLOT_P + q] = rows


def expert_kernel(x_ref, up_ref, down_ref, out_ref):
    parts, clips, width = x_ref.shape
    x = x_ref[...].astype(F32).reshape(parts * clips, width).astype(BF16)
    hidden = jax.nn.gelu(jnp.dot(x, up_ref[...], preferred_element_type=F32)).astype(BF16)
    out = jnp.dot(hidden, down_ref[...], preferred_element_type=F32)
    out_ref[...] = out.reshape(parts, clips, width).astype(BF16)


def total_kernel(x_ref, out_ref):
    parts, clips, width = x_ref.shape
    x = x_ref[...].astype(F32).reshape(parts // SLOT_P, SLOT_P, clips, width)
    total = jnp.sum(x, axis=1)
    for c in range(clips):
        rows = jnp.concatenate([total[g, c : c + 1] for g in range(parts // SLOT_P)], axis=0).astype(BF16)
        for k in range(out_ref.shape[0]):
            out_ref[k, c] = rows


def split_kernel(in_ref, *out_refs):
    nz, _, groups, width = in_ref.shape
    for c, ref in enumerate(out_refs):
        ref[...] = in_ref[:, c].astype(F32).reshape(nz * groups, width).astype(BF16)


def mix_kernel(clip, ny, comb_ref, *refs):
    slot_refs, (out_hbm, held, buf, sems) = refs[:ny], refs[-4:]
    rows = slot_refs[0].shape[0]
    for i, r in zip(FAR_LAST, slot_refs):
        held[i * rows : (i + 1) * rows] = r[...]
    step = buf.shape[0] // STEPS
    copies = []
    for i in range(STEPS):
        part = pl.ds(i * step, step)
        buf[part] = jnp.dot(comb_ref[part], held[...], preferred_element_type=F32).astype(BF16)
        copies.append(pltpu.make_async_copy(buf.at[part], out_hbm.at[clip, part], sems.at[i]))
        copies[-1].start()
    for copy in copies:
        copy.wait()


def shards(tokens, slot_params, w_up, w_down):
    clips, length, width = tokens.shape
    slots = slot_params.shape[1]
    groups = lax.axis_size("group")
    around = ("zh", "quarter")
    ny, nz = lax.axis_size("y"), lax.axis_size(around)
    sharers = ("group", "quarter")
    wide = width + STAT

    def shift(x, k):
        return lax.ppermute(x, "y", [(i, (i + k) % ny) for i in range(ny)])

    def small(kernel, out, label, *operands):
        return pl.pallas_call(
            kernel,
            in_specs=[vmem()] * len(operands),
            out_specs=jax.tree.map(lambda _: vmem(), out),
            out_shape=out,
            compiler_params=params(),
            name=label,
        )(*operands)

    def gather(clip, sp):
        extra = [jax.ShapeDtypeStruct((width, slots), BF16)] if clip == 0 else []
        return pl.pallas_call(
            name(gather_kernel, clip, groups, ny, nz),
            in_specs=[anywhere(), anywhere()] if clip == 0 else [vmem(), vmem()],
            out_specs=[vmem()] * (ny + len(extra)),
            out_shape=[jax.ShapeDtypeStruct((nz * groups * (width // LANES) + STAT_ROWS, LANES), BF16)] * ny + extra,
            scratch_shapes=[
                pltpu.VMEM((width, slots), BF16),
                pltpu.VMEM((length, width), BF16),
                pltpu.VMEM((length, slots), F32),
                pltpu.SemaphoreType.DMA((STEPS + PIECES,)),
            ]
            if clip == 0
            else [pltpu.VMEM((length, slots), F32)],
            compiler_params=params(BIG + 0.625 if clip == 0 else LATE),
            cost_estimate=pl.CostEstimate(
                flops=4 * length * width * slots,
                bytes_accessed=2 * length * width,
                transcendentals=length * slots,
            ),
            name=f"gather{clip}",
        )(tokens, sp)

    def combine(clip, after):
        half = length // 2
        return pl.pallas_call(
            combine_kernel,
            grid=(2,),
            in_specs=[
                pl.BlockSpec((1, half, width), lambda t: (clip, t, 0)),
                pl.BlockSpec((width, slots), lambda t: (0, 0)),
                pl.BlockSpec((1,) * (after.ndim - 2) + (8, STAT), lambda t: (0,) * after.ndim),
            ],
            out_specs=[
                pl.BlockSpec((half, slots), lambda t: (t, 0)),
                pl.BlockSpec((8, STAT), lambda t: (0, 0)),
            ],
            out_shape=[
                jax.ShapeDtypeStruct((length, slots), BF16),
                jax.ShapeDtypeStruct((8, STAT), F32),
            ],
            compiler_params=params(LATE),
            cost_estimate=pl.CostEstimate(
                flops=2 * length * width * slots,
                bytes_accessed=2 * length * (width + slots),
                transcendentals=length * slots,
            ),
            name=f"combine{clip}",
        )(tokens, ordered, after)

    assert clips == 2 and ny == 4
    *means0, ordered = gather(0, slot_params)
    sent0 = {k: shift(means0[k], k) for k in FAR_FIRST}
    means1 = gather(1, ordered)
    sent1 = {k: shift(means1[k], k) for k in FAR_FIRST}
    arrived = [means0[0], *sent0.values(), means1[0], *sent1.values()]
    combine0, tick = combine(0, means1[0])
    combine1, tick = combine(1, tick)
    halfway = small(
        halfway_kernel,
        jax.ShapeDtypeStruct((nz, groups, wide), BF16),
        "halfway",
        *arrived[:ny],
        tick,
    )
    halfway = small(
        both_kernel,
        jax.ShapeDtypeStruct((nz, clips, groups, wide), BF16),
        "both",
        *arrived[ny:],
        halfway,
    )
    arrived = lax.all_to_all(halfway, around, 0, 0, tiled=True)
    rows = jax.ShapeDtypeStruct((groups * SLOT_P, clips, width), BF16)
    slot_in = small(name(merge_kernel, width), rows, "merge", arrived)
    own = lax.all_to_all(slot_in, sharers, 0, 0, tiled=True)
    partial = small(expert_kernel, rows, "expert", own, w_up, w_down)
    back = lax.all_to_all(partial, sharers, 0, 0, tiled=True)
    slot_out = small(
        total_kernel, jax.ShapeDtypeStruct((nz, clips, groups, width), BF16), "total", back
    )
    ring = lax.all_to_all(slot_out, around, 0, 0, tiled=True)
    rings = small(
        split_kernel, [jax.ShapeDtypeStruct((nz * groups, width), BF16)] * clips, "split", ring
    )
    combines = [combine0, combine1]
    rings = [[shift(ring, -k) if k else ring for k in FAR_LAST] for ring in rings]
    mixed = None
    for clip in range(clips):
        before = [] if mixed is None else [mixed]
        mixed = pl.pallas_call(
            name(mix_kernel, clip, ny),
            in_specs=[vmem()] * (1 + ny) + [anywhere() for _ in before],
            out_specs=anywhere(),
            out_shape=jax.ShapeDtypeStruct((clips, length, width), BF16),
            scratch_shapes=[
                pltpu.VMEM((slots, width), BF16),
                pltpu.VMEM((length, width), BF16),
                pltpu.SemaphoreType.DMA((STEPS,)),
            ],
            input_output_aliases={1 + ny: 0} if before else {},
            compiler_params=params(),
            cost_estimate=pl.CostEstimate(
                flops=2 * length * width * slots,
                bytes_accessed=2 * length * (width + slots),
                transcendentals=0,
            ),
            name=f"mix{clip}",
        )(combines[clip], *rings[clip], *before)
    return mixed


def solution(mesh):
    groups, n = mesh.devices.shape
    split = Mesh(mesh.devices.reshape(groups, 4, n // (4 * SLOT_P), SLOT_P), ("group", "y", "zh", "quarter"))
    seq = ("y", "zh", "quarter")
    everyone = ("group",) + seq
    placed = (P("group", seq, None), P(), P(None, everyone), P(everyone, None))
    return jax.shard_map(
        shards, mesh=split, in_specs=placed, out_specs=P("group", seq, None), check_vma=False
    )
```

```python
import functools

import jax
import jax.numpy as jnp
from jax import lax
from jax.experimental import pallas as pl
from jax.experimental.pallas import tpu as pltpu
from jax.sharding import Mesh
from jax.sharding import PartitionSpec as P

F32 = jnp.float32
BF16 = jnp.bfloat16
SLOT_P = 4
LANES = 128
STAT = LANES
STAT_ROWS = 16
FETCHES = 2
STEPS = 4
MIB = 1 << 20
BIG = 52
LATE = 44
FAR_FIRST = (2, 1, 3)
FAR_LAST = (0, 1, 3, 2)


def vmem():
    return pl.BlockSpec(memory_space=pltpu.VMEM)


def anywhere():
    return pl.BlockSpec(memory_space=pl.ANY)


def params(mib=48):
    return pltpu.CompilerParams(vmem_limit_bytes=int(mib * MIB))


def name(f, *a):
    def body(*refs):
        f(*a, *refs)

    return body


def device_order(slots, groups, ny, nz):
    col = lax.broadcasted_iota(jnp.int32, (1, slots), 1)
    at_y = (col // (nz * groups) + lax.axis_index("y")) % ny
    slot = (col % groups * ny + at_y) * nz + col // groups % nz
    return (lax.broadcasted_iota(jnp.int32, (slots, slots), 0) == slot).astype(F32).astype(BF16)


def thirds(lse):
    hi = lse.astype(BF16).astype(F32)
    mid = (lse - hi).astype(BF16).astype(F32)
    return hi, mid, lse - hi - mid


def pack(lse):
    hi, mid, low = thirds(lse)
    lane = lax.broadcasted_iota(jnp.int32, lse.shape[:-1] + (STAT,), lse.ndim - 1)
    return jnp.where(lane == 0, hi, jnp.where(lane == 1, mid, jnp.where(lane == 2, low, 0.0)))


def gather_kernel(clip, groups, ny, nz, tok_in, sp_ref, *refs):
    out_refs, refs = refs[:ny], refs[ny:]
    copies = []
    parts = FETCHES if clip == 0 else STEPS
    if clip == 0:
        ordered_ref, raw_ref, tok_ref, logit_ref, sems = refs
        rows = tok_ref.shape[0] // parts
        first = pltpu.make_async_copy(sp_ref, raw_ref, sems.at[parts])
        first.start()
        for i in range(parts):
            part = pl.ds(i * rows, rows)
            copies.append(pltpu.make_async_copy(tok_in.at[clip, part], tok_ref.at[part], sems.at[i]))
            copies[-1].start()
        perm = device_order(raw_ref.shape[1], groups, ny, nz)
        first.wait()
        ordered_ref[...] = jnp.dot(raw_ref[...], perm, preferred_element_type=F32).astype(BF16)
    else:
        ordered_ref, tok_ref, logit_ref = sp_ref, tok_in.at[clip], refs[0]
        rows = tok_ref.shape[0] // parts
    peak = None
    for i in range(parts):
        if copies:
            copies[i].wait()
        part = slice(i * rows, (i + 1) * rows)
        logits = jnp.dot(tok_ref[part], ordered_ref[...], preferred_element_type=F32)
        logit_ref[part] = logits
        top = jnp.max(logits, axis=0, keepdims=True)
        peak = top if peak is None else jnp.maximum(peak, top)
    spread = jnp.exp(logit_ref[...] - peak)
    total = jnp.sum(spread, axis=0, keepdims=True)
    summed = lax.dot_general(
        spread.astype(BF16), tok_ref[...], (((0,), (0,)), ((), ())), preferred_element_type=F32
    )
    slots = total.shape[1]
    cols = jnp.concatenate([1.0 / total, jnp.zeros((7, slots), F32)], axis=0).T
    mean = (summed * cols[:, 0:1]).astype(BF16)
    stat = jnp.concatenate([*thirds(peak + jnp.log(total)), jnp.zeros((13, slots), F32)], axis=0).astype(BF16)
    rows = nz * groups
    for i in range(ny):
        block = mean[i * rows : (i + 1) * rows]
        tiles = block.shape[1] // LANES
        for t in range(tiles):
            out_refs[i][t * rows : (t + 1) * rows] = block[:, t * LANES : (t + 1) * LANES]
        at = i * rows // LANES * LANES
        out_refs[i][tiles * rows :] = stat[:, at : at + LANES]


def combine_kernel(tok_ref, sp_ref, after_ref, out_ref, tick_ref):
    logits = jnp.dot(tok_ref[0], sp_ref[...], preferred_element_type=F32)
    spread = jnp.exp(logits - jnp.max(logits, axis=1, keepdims=True))
    out_ref[...] = (spread * (1.0 / jnp.sum(spread, axis=1, keepdims=True))).astype(BF16)
    tick_ref[...] = jnp.zeros_like(tick_ref)


def merged(width, wides):
    lses = []
    for wide in wides:
        stat = wide[..., width:].astype(F32)
        lses.append(stat[..., 0:1] + stat[..., 1:2] + stat[..., 2:3])
    peak = functools.reduce(jnp.maximum, lses)
    weights = [jnp.exp(lse - peak) for lse in lses]
    total = sum(weights)
    mean = sum(wide[..., :width].astype(F32) * (w / total) for wide, w in zip(wides, weights))
    return mean, peak + jnp.log(total)


def along_y(rows, in_refs, store):
    tiles = (in_refs[0].shape[0] - STAT_ROWS) // rows
    lses = []
    for k, ref in zip((0,) + FAR_FIRST, in_refs):
        at = k * rows % LANES
        stat = ref[tiles * rows :].astype(F32).T[at : at + rows]
        lses.append(stat[:, 0:1] + stat[:, 1:2] + stat[:, 2:3])
    peak = functools.reduce(jnp.maximum, lses)
    weights = [jnp.exp(lse - peak) for lse in lses]
    total = sum(weights)
    weights = [w / total for w in weights]
    for t in range(tiles):
        part = slice(t * rows, (t + 1) * rows)
        store(t, sum(ref[part].astype(F32) * w for ref, w in zip(in_refs, weights)))
    store(tiles, pack(peak + jnp.log(total)))


def halfway_kernel(*refs):
    in_refs, out_ref = refs[:-2], refs[-1]
    nz, groups = out_ref.shape[:2]

    def store(t, x):
        out_ref[:, :, t * LANES : (t + 1) * LANES] = x.reshape(nz, groups, LANES).astype(BF16)

    along_y(nz * groups, in_refs, store)


def both_kernel(*refs):
    in_refs, first_ref, out_ref = refs[:-2], refs[-2], refs[-1]
    nz, _, groups = out_ref.shape[:3]

    def store(t, x):
        out_ref[:, 1, :, t * LANES : (t + 1) * LANES] = x.reshape(nz, groups, LANES).astype(BF16)

    out_ref[:, 0] = first_ref[...]
    along_y(nz * groups, in_refs, store)


def merge_kernel(width, in_ref, out_ref):
    nz, clips, groups = in_ref.shape[:3]
    acc, _ = merged(width, [in_ref[k] for k in range(nz)])
    for g in range(groups):
        rows = jnp.concatenate([acc[c, g : g + 1] for c in range(clips)], axis=0).astype(BF16)
        for q in range(SLOT_P):
            out_ref[g * SLOT_P + q] = rows


def expert_kernel(x_ref, up_ref, down_ref, out_ref):
    parts, clips, width = x_ref.shape
    x = x_ref[...].astype(F32).reshape(parts * clips, width).astype(BF16)
    hidden = jax.nn.gelu(jnp.dot(x, up_ref[...], preferred_element_type=F32)).astype(BF16)
    out = jnp.dot(hidden, down_ref[...], preferred_element_type=F32)
    out_ref[...] = out.reshape(parts, clips, width).astype(BF16)


def total_kernel(x_ref, out_ref):
    parts, clips, width = x_ref.shape
    x = x_ref[...].astype(F32).reshape(parts // SLOT_P, SLOT_P, clips, width)
    total = jnp.sum(x, axis=1)
    for c in range(clips):
        rows = jnp.concatenate([total[g, c : c + 1] for g in range(parts // SLOT_P)], axis=0).astype(BF16)
        for k in range(out_ref.shape[0]):
            out_ref[k, c] = rows


def split_kernel(in_ref, *out_refs):
    nz, _, groups, width = in_ref.shape
    for c, ref in enumerate(out_refs):
        ref[...] = in_ref[:, c].astype(F32).reshape(nz * groups, width).astype(BF16)


def mix_kernel(clip, ny, comb_ref, *refs):
    slot_refs, (out_hbm, held, buf, sems) = refs[:ny], refs[-4:]
    rows = slot_refs[0].shape[0]
    for i, r in zip(FAR_LAST, slot_refs):
        held[i * rows : (i + 1) * rows] = r[...]
    step = buf.shape[0] // STEPS
    copies = []
    for i in range(STEPS):
        part = pl.ds(i * step, step)
        buf[part] = jnp.dot(comb_ref[part], held[...], preferred_element_type=F32).astype(BF16)
        copies.append(pltpu.make_async_copy(buf.at[part], out_hbm.at[clip, part], sems.at[i]))
        copies[-1].start()
    for copy in copies:
        copy.wait()


def shards(tokens, slot_params, w_up, w_down):
    clips, length, width = tokens.shape
    slots = slot_params.shape[1]
    groups = lax.axis_size("group")
    around = ("zh", "quarter")
    ny, nz = lax.axis_size("y"), lax.axis_size(around)
    sharers = ("group", "quarter")
    wide = width + STAT

    def shift(x, k):
        return lax.ppermute(x, "y", [(i, (i + k) % ny) for i in range(ny)])

    def small(kernel, out, label, *operands):
        return pl.pallas_call(
            kernel,
            in_specs=[vmem()] * len(operands),
            out_specs=jax.tree.map(lambda _: vmem(), out),
            out_shape=out,
            compiler_params=params(),
            name=label,
        )(*operands)

    def gather(clip, sp):
        extra = [jax.ShapeDtypeStruct((width, slots), BF16)] if clip == 0 else []
        return pl.pallas_call(
            name(gather_kernel, clip, groups, ny, nz),
            in_specs=[anywhere(), anywhere()] if clip == 0 else [vmem(), vmem()],
            out_specs=[vmem()] * (ny + len(extra)),
            out_shape=[jax.ShapeDtypeStruct((nz * groups * (width // LANES) + STAT_ROWS, LANES), BF16)] * ny + extra,
            scratch_shapes=[
                pltpu.VMEM((width, slots), BF16),
                pltpu.VMEM((length, width), BF16),
                pltpu.VMEM((length, slots), F32),
                pltpu.SemaphoreType.DMA((FETCHES + 1,)),
            ]
            if clip == 0
            else [pltpu.VMEM((length, slots), F32)],
            compiler_params=params(BIG + 0.625 if clip == 0 else LATE),
            cost_estimate=pl.CostEstimate(
                flops=4 * length * width * slots,
                bytes_accessed=2 * length * width,
                transcendentals=length * slots,
            ),
            name=f"gather{clip}",
        )(tokens, sp)

    def combine(clip, after):
        half = length // 2
        return pl.pallas_call(
            combine_kernel,
            grid=(2,),
            in_specs=[
                pl.BlockSpec((1, half, width), lambda t: (clip, t, 0)),
                pl.BlockSpec((width, slots), lambda t: (0, 0)),
                pl.BlockSpec((1,) * (after.ndim - 2) + (8, STAT), lambda t: (0,) * after.ndim),
            ],
            out_specs=[
                pl.BlockSpec((half, slots), lambda t: (t, 0)),
                pl.BlockSpec((8, STAT), lambda t: (0, 0)),
            ],
            out_shape=[
                jax.ShapeDtypeStruct((length, slots), BF16),
                jax.ShapeDtypeStruct((8, STAT), F32),
            ],
            compiler_params=params(LATE),
            cost_estimate=pl.CostEstimate(
                flops=2 * length * width * slots,
                bytes_accessed=2 * length * (width + slots),
                transcendentals=length * slots,
            ),
            name=f"combine{clip}",
        )(tokens, ordered, after)

    assert clips == 2 and ny == 4
    *means0, ordered = gather(0, slot_params)
    sent0 = {k: shift(means0[k], k) for k in FAR_FIRST}
    means1 = gather(1, ordered)
    sent1 = {k: shift(means1[k], k) for k in FAR_FIRST}
    arrived = [means0[0], *sent0.values(), means1[0], *sent1.values()]
    combine0, tick = combine(0, means1[0])
    combine1, tick = combine(1, tick)
    halfway = small(
        halfway_kernel,
        jax.ShapeDtypeStruct((nz, groups, wide), BF16),
        "halfway",
        *arrived[:ny],
        tick,
    )
    halfway = small(
        both_kernel,
        jax.ShapeDtypeStruct((nz, clips, groups, wide), BF16),
        "both",
        *arrived[ny:],
        halfway,
    )
    arrived = lax.all_to_all(halfway, around, 0, 0, tiled=True)
    rows = jax.ShapeDtypeStruct((groups * SLOT_P, clips, width), BF16)
    slot_in = small(name(merge_kernel, width), rows, "merge", arrived)
    own = lax.all_to_all(slot_in, sharers, 0, 0, tiled=True)
    partial = small(expert_kernel, rows, "expert", own, w_up, w_down)
    back = lax.all_to_all(partial, sharers, 0, 0, tiled=True)
    slot_out = small(
        total_kernel, jax.ShapeDtypeStruct((nz, clips, groups, width), BF16), "total", back
    )
    ring = lax.all_to_all(slot_out, around, 0, 0, tiled=True)
    rings = small(
        split_kernel, [jax.ShapeDtypeStruct((nz * groups, width), BF16)] * clips, "split", ring
    )
    combines = [combine0, combine1]
    rings = [[shift(ring, -k) if k else ring for k in FAR_LAST] for ring in rings]
    mixed = None
    for clip in range(clips):
        before = [] if mixed is None else [mixed]
        mixed = pl.pallas_call(
            name(mix_kernel, clip, ny),
            in_specs=[vmem()] * (1 + ny) + [anywhere() for _ in before],
            out_specs=anywhere(),
            out_shape=jax.ShapeDtypeStruct((clips, length, width), BF16),
            scratch_shapes=[
                pltpu.VMEM((slots, width), BF16),
                pltpu.VMEM((length, width), BF16),
                pltpu.SemaphoreType.DMA((STEPS,)),
            ],
            input_output_aliases={1 + ny: 0} if before else {},
            compiler_params=params(),
            cost_estimate=pl.CostEstimate(
                flops=2 * length * width * slots,
                bytes_accessed=2 * length * (width + slots),
                transcendentals=0,
            ),
            name=f"mix{clip}",
        )(combines[clip], *rings[clip], *before)
    return mixed


def solution(mesh):
    groups, n = mesh.devices.shape
    split = Mesh(mesh.devices.reshape(groups, 4, n // (4 * SLOT_P), SLOT_P), ("group", "y", "zh", "quarter"))
    seq = ("y", "zh", "quarter")
    everyone = ("group",) + seq
    placed = (P("group", seq, None), P(), P(None, everyone), P(everyone, None))
    return jax.shard_map(
        shards, mesh=split, in_specs=placed, out_specs=P("group", seq, None), check_vma=False
    )
```

```python
import functools

import jax
import jax.numpy as jnp
from jax import lax
from jax.experimental import pallas as pl
from jax.experimental.pallas import tpu as pltpu
from jax.sharding import Mesh
from jax.sharding import PartitionSpec as P

F32 = jnp.float32
BF16 = jnp.bfloat16
SLOT_P = 4
LANES = 128
STAT = LANES
STAT_ROWS = 16
FETCHES = 1
STEPS = 4
MIB = 1 << 20
BIG = 52
LATE = 44
FAR_FIRST = (2, 1, 3)
FAR_LAST = (0, 1, 3, 2)


def vmem():
    return pl.BlockSpec(memory_space=pltpu.VMEM)


def anywhere():
    return pl.BlockSpec(memory_space=pl.ANY)


def params(mib=48):
    return pltpu.CompilerParams(vmem_limit_bytes=int(mib * MIB))


def name(f, *a):
    def body(*refs):
        f(*a, *refs)

    return body


def device_order(slots, groups, ny, nz):
    col = lax.broadcasted_iota(jnp.int32, (1, slots), 1)
    at_y = (col // (nz * groups) + lax.axis_index("y")) % ny
    slot = (col % groups * ny + at_y) * nz + col // groups % nz
    return (lax.broadcasted_iota(jnp.int32, (slots, slots), 0) == slot).astype(F32).astype(BF16)


def thirds(lse):
    hi = lse.astype(BF16).astype(F32)
    mid = (lse - hi).astype(BF16).astype(F32)
    return hi, mid, lse - hi - mid


def pack(lse):
    hi, mid, low = thirds(lse)
    lane = lax.broadcasted_iota(jnp.int32, lse.shape[:-1] + (STAT,), lse.ndim - 1)
    return jnp.where(lane == 0, hi, jnp.where(lane == 1, mid, jnp.where(lane == 2, low, 0.0)))


def gather_kernel(clip, groups, ny, nz, tok_in, sp_ref, *refs):
    out_refs, refs = refs[:ny], refs[ny:]
    copies = []
    parts = FETCHES if clip == 0 else STEPS
    if clip == 0:
        ordered_ref, raw_ref, tok_ref, logit_ref, sems = refs
        rows = tok_ref.shape[0] // parts
        first = pltpu.make_async_copy(sp_ref, raw_ref, sems.at[parts])
        first.start()
        for i in range(parts):
            part = pl.ds(i * rows, rows)
            copies.append(pltpu.make_async_copy(tok_in.at[clip, part], tok_ref.at[part], sems.at[i]))
            copies[-1].start()
        perm = device_order(raw_ref.shape[1], groups, ny, nz)
        first.wait()
        ordered_ref[...] = jnp.dot(raw_ref[...], perm, preferred_element_type=F32).astype(BF16)
    else:
        ordered_ref, tok_ref, logit_ref = sp_ref, tok_in.at[clip], refs[0]
        rows = tok_ref.shape[0] // parts
    peak = None
    for i in range(parts):
        if copies:
            copies[i].wait()
        part = slice(i * rows, (i + 1) * rows)
        logits = jnp.dot(tok_ref[part], ordered_ref[...], preferred_element_type=F32)
        logit_ref[part] = logits
        top = jnp.max(logits, axis=0, keepdims=True)
        peak = top if peak is None else jnp.maximum(peak, top)
    spread = jnp.exp(logit_ref[...] - peak)
    total = jnp.sum(spread, axis=0, keepdims=True)
    summed = lax.dot_general(
        spread.astype(BF16), tok_ref[...], (((0,), (0,)), ((), ())), preferred_element_type=F32
    )
    slots = total.shape[1]
    cols = jnp.concatenate([1.0 / total, jnp.zeros((7, slots), F32)], axis=0).T
    mean = (summed * cols[:, 0:1]).astype(BF16)
    stat = jnp.concatenate([*thirds(peak + jnp.log(total)), jnp.zeros((13, slots), F32)], axis=0).astype(BF16)
    rows = nz * groups
    for i in range(ny):
        block = mean[i * rows : (i + 1) * rows]
        tiles = block.shape[1] // LANES
        for t in range(tiles):
            out_refs[i][t * rows : (t + 1) * rows] = block[:, t * LANES : (t + 1) * LANES]
        at = i * rows // LANES * LANES
        out_refs[i][tiles * rows :] = stat[:, at : at + LANES]


def combine_kernel(tok_ref, sp_ref, after_ref, out_ref, tick_ref):
    logits = jnp.dot(tok_ref[0], sp_ref[...], preferred_element_type=F32)
    spread = jnp.exp(logits - jnp.max(logits, axis=1, keepdims=True))
    out_ref[...] = (spread * (1.0 / jnp.sum(spread, axis=1, keepdims=True))).astype(BF16)
    tick_ref[...] = jnp.zeros_like(tick_ref)


def merged(width, wides):
    lses = []
    for wide in wides:
        stat = wide[..., width:].astype(F32)
        lses.append(stat[..., 0:1] + stat[..., 1:2] + stat[..., 2:3])
    peak = functools.reduce(jnp.maximum, lses)
    weights = [jnp.exp(lse - peak) for lse in lses]
    total = sum(weights)
    mean = sum(wide[..., :width].astype(F32) * (w / total) for wide, w in zip(wides, weights))
    return mean, peak + jnp.log(total)


def along_y(rows, in_refs, store):
    tiles = (in_refs[0].shape[0] - STAT_ROWS) // rows
    lses = []
    for k, ref in zip((0,) + FAR_FIRST, in_refs):
        at = k * rows % LANES
        stat = ref[tiles * rows :].astype(F32).T[at : at + rows]
        lses.append(stat[:, 0:1] + stat[:, 1:2] + stat[:, 2:3])
    peak = functools.reduce(jnp.maximum, lses)
    weights = [jnp.exp(lse - peak) for lse in lses]
    total = sum(weights)
    weights = [w / total for w in weights]
    for t in range(tiles):
        part = slice(t * rows, (t + 1) * rows)
        store(t, sum(ref[part].astype(F32) * w for ref, w in zip(in_refs, weights)))
    store(tiles, pack(peak + jnp.log(total)))


def halfway_kernel(*refs):
    in_refs, out_ref = refs[:-2], refs[-1]
    nz, groups = out_ref.shape[:2]

    def store(t, x):
        out_ref[:, :, t * LANES : (t + 1) * LANES] = x.reshape(nz, groups, LANES).astype(BF16)

    along_y(nz * groups, in_refs, store)


def both_kernel(*refs):
    in_refs, first_ref, out_ref = refs[:-2], refs[-2], refs[-1]
    nz, _, groups = out_ref.shape[:3]

    def store(t, x):
        out_ref[:, 1, :, t * LANES : (t + 1) * LANES] = x.reshape(nz, groups, LANES).astype(BF16)

    out_ref[:, 0] = first_ref[...]
    along_y(nz * groups, in_refs, store)


def merge_kernel(width, in_ref, out_ref):
    nz, clips, groups = in_ref.shape[:3]
    acc, _ = merged(width, [in_ref[k] for k in range(nz)])
    for g in range(groups):
        rows = jnp.concatenate([acc[c, g : g + 1] for c in range(clips)], axis=0).astype(BF16)
        for q in range(SLOT_P):
            out_ref[g * SLOT_P + q] = rows


def expert_kernel(x_ref, up_ref, down_ref, out_ref):
    parts, clips, width = x_ref.shape
    x = x_ref[...].astype(F32).reshape(parts * clips, width).astype(BF16)
    hidden = jax.nn.gelu(jnp.dot(x, up_ref[...], preferred_element_type=F32)).astype(BF16)
    out = jnp.dot(hidden, down_ref[...], preferred_element_type=F32)
    out_ref[...] = out.reshape(parts, clips, width).astype(BF16)


def total_kernel(x_ref, out_ref):
    parts, clips, width = x_ref.shape
    x = x_ref[...].astype(F32).reshape(parts // SLOT_P, SLOT_P, clips, width)
    total = jnp.sum(x, axis=1)
    for c in range(clips):
        rows = jnp.concatenate([total[g, c : c + 1] for g in range(parts // SLOT_P)], axis=0).astype(BF16)
        for k in range(out_ref.shape[0]):
            out_ref[k, c] = rows


def split_kernel(in_ref, *out_refs):
    nz, _, groups, width = in_ref.shape
    for c, ref in enumerate(out_refs):
        ref[...] = in_ref[:, c].astype(F32).reshape(nz * groups, width).astype(BF16)


def mix_kernel(clip, ny, comb_ref, *refs):
    slot_refs, (out_hbm, held, buf, sems) = refs[:ny], refs[-4:]
    rows = slot_refs[0].shape[0]
    for i, r in zip(FAR_LAST, slot_refs):
        held[i * rows : (i + 1) * rows] = r[...]
    step = buf.shape[0] // STEPS
    copies = []
    for i in range(STEPS):
        part = pl.ds(i * step, step)
        buf[part] = jnp.dot(comb_ref[part], held[...], preferred_element_type=F32).astype(BF16)
        copies.append(pltpu.make_async_copy(buf.at[part], out_hbm.at[clip, part], sems.at[i]))
        copies[-1].start()
    for copy in copies:
        copy.wait()


def shards(tokens, slot_params, w_up, w_down):
    clips, length, width = tokens.shape
    slots = slot_params.shape[1]
    groups = lax.axis_size("group")
    around = ("zh", "quarter")
    ny, nz = lax.axis_size("y"), lax.axis_size(around)
    sharers = ("group", "quarter")
    wide = width + STAT

    def shift(x, k):
        return lax.ppermute(x, "y", [(i, (i + k) % ny) for i in range(ny)])

    def small(kernel, out, label, *operands):
        return pl.pallas_call(
            kernel,
            in_specs=[vmem()] * len(operands),
            out_specs=jax.tree.map(lambda _: vmem(), out),
            out_shape=out,
            compiler_params=params(),
            name=label,
        )(*operands)

    def gather(clip, sp):
        extra = [jax.ShapeDtypeStruct((width, slots), BF16)] if clip == 0 else []
        return pl.pallas_call(
            name(gather_kernel, clip, groups, ny, nz),
            in_specs=[anywhere(), anywhere()] if clip == 0 else [vmem(), vmem()],
            out_specs=[vmem()] * (ny + len(extra)),
            out_shape=[jax.ShapeDtypeStruct((nz * groups * (width // LANES) + STAT_ROWS, LANES), BF16)] * ny + extra,
            scratch_shapes=[
                pltpu.VMEM((width, slots), BF16),
                pltpu.VMEM((length, width), BF16),
                pltpu.VMEM((length, slots), F32),
                pltpu.SemaphoreType.DMA((FETCHES + 1,)),
            ]
            if clip == 0
            else [pltpu.VMEM((length, slots), F32)],
            compiler_params=params(BIG + 0.625 if clip == 0 else LATE),
            cost_estimate=pl.CostEstimate(
                flops=4 * length * width * slots,
                bytes_accessed=2 * length * width,
                transcendentals=length * slots,
            ),
            name=f"gather{clip}",
        )(tokens, sp)

    def combine(clip, after):
        half = length // 2
        return pl.pallas_call(
            combine_kernel,
            grid=(2,),
            in_specs=[
                pl.BlockSpec((1, half, width), lambda t: (clip, t, 0)),
                pl.BlockSpec((width, slots), lambda t: (0, 0)),
                pl.BlockSpec((1,) * (after.ndim - 2) + (8, STAT), lambda t: (0,) * after.ndim),
            ],
            out_specs=[
                pl.BlockSpec((half, slots), lambda t: (t, 0)),
                pl.BlockSpec((8, STAT), lambda t: (0, 0)),
            ],
            out_shape=[
                jax.ShapeDtypeStruct((length, slots), BF16),
                jax.ShapeDtypeStruct((8, STAT), F32),
            ],
            compiler_params=params(LATE),
            cost_estimate=pl.CostEstimate(
                flops=2 * length * width * slots,
                bytes_accessed=2 * length * (width + slots),
                transcendentals=length * slots,
            ),
            name=f"combine{clip}",
        )(tokens, ordered, after)

    assert clips == 2 and ny == 4
    *means0, ordered = gather(0, slot_params)
    sent0 = {k: shift(means0[k], k) for k in FAR_FIRST}
    means1 = gather(1, ordered)
    sent1 = {k: shift(means1[k], k) for k in FAR_FIRST}
    arrived = [means0[0], *sent0.values(), means1[0], *sent1.values()]
    combine0, tick = combine(0, means1[0])
    combine1, tick = combine(1, tick)
    halfway = small(
        halfway_kernel,
        jax.ShapeDtypeStruct((nz, groups, wide), BF16),
        "halfway",
        *arrived[:ny],
        tick,
    )
    halfway = small(
        both_kernel,
        jax.ShapeDtypeStruct((nz, clips, groups, wide), BF16),
        "both",
        *arrived[ny:],
        halfway,
    )
    arrived = lax.all_to_all(halfway, around, 0, 0, tiled=True)
    rows = jax.ShapeDtypeStruct((groups * SLOT_P, clips, width), BF16)
    slot_in = small(name(merge_kernel, width), rows, "merge", arrived)
    own = lax.all_to_all(slot_in, sharers, 0, 0, tiled=True)
    partial = small(expert_kernel, rows, "expert", own, w_up, w_down)
    back = lax.all_to_all(partial, sharers, 0, 0, tiled=True)
    slot_out = small(
        total_kernel, jax.ShapeDtypeStruct((nz, clips, groups, width), BF16), "total", back
    )
    ring = lax.all_to_all(slot_out, around, 0, 0, tiled=True)
    rings = small(
        split_kernel, [jax.ShapeDtypeStruct((nz * groups, width), BF16)] * clips, "split", ring
    )
    combines = [combine0, combine1]
    rings = [[shift(ring, -k) if k else ring for k in FAR_LAST] for ring in rings]
    mixed = None
    for clip in range(clips):
        before = [] if mixed is None else [mixed]
        mixed = pl.pallas_call(
            name(mix_kernel, clip, ny),
            in_specs=[vmem()] * (1 + ny) + [anywhere() for _ in before],
            out_specs=anywhere(),
            out_shape=jax.ShapeDtypeStruct((clips, length, width), BF16),
            scratch_shapes=[
                pltpu.VMEM((slots, width), BF16),
                pltpu.VMEM((length, width), BF16),
                pltpu.SemaphoreType.DMA((STEPS,)),
            ],
            input_output_aliases={1 + ny: 0} if before else {},
            compiler_params=params(),
            cost_estimate=pl.CostEstimate(
                flops=2 * length * width * slots,
                bytes_accessed=2 * length * (width + slots),
                transcendentals=0,
            ),
            name=f"mix{clip}",
        )(combines[clip], *rings[clip], *before)
    return mixed


def solution(mesh):
    groups, n = mesh.devices.shape
    split = Mesh(mesh.devices.reshape(groups, 4, n // (4 * SLOT_P), SLOT_P), ("group", "y", "zh", "quarter"))
    seq = ("y", "zh", "quarter")
    everyone = ("group",) + seq
    placed = (P("group", seq, None), P(), P(None, everyone), P(everyone, None))
    return jax.shard_map(
        shards, mesh=split, in_specs=placed, out_specs=P("group", seq, None), check_vma=False
    )
```
